512 devices in a mesh: gx: 8 (over y), gy: 16 (over z, core), gz: 4 (over x).
Axes of the slice: x: 4, y: 8, z: 8, core: 2. Of those that a mesh axis runs over, the one named last changes fastest.
Arguments:
- positions: float32 [8, 16, 4, 3, 1024], P('gx', 'gy', 'gz'), may hold values from 0 to 21.7, as said below
- polar: float32 [8, 16, 4, 1024], P('gx', 'gy', 'gz'), may hold values from 0.4 to 3
- field: float32 [8, 16, 4, 3, 1024], P('gx', 'gy', 'gz'), may hold values from -24 to 24
- groups: int32 [8, 16, 4, 1024], P('gx', 'gy', 'gz'), may hold values from 0 to 255, never falling along the last dimension, each value on 1 to 8 neighbouring positions
- pair_tiles: int32 [8, 16, 4, 3, 112], P('gx', 'gy', 'gz'), may hold values from 0 to 14, as said below
Outputs:
- dipoles: float32 [8, 16, 4, 3, 1024], P('gx', 'gy', 'gz')
- residual: float32 [8, 16, 4, 3, 1024], P('gx', 'gy', 'gz')
The draws below stay inside these ranges and needn't reach their ends.
Inputs may be any that keep to these rules, and one draw needn't show every extreme that they name: `positions`: atom k of tile t of a device lies in the sub-box (t // 4, t // 2 % 2, t % 2) of edge 10.85 of the device's block, near a lattice site of that sub-box; two atoms are never closer than 0.6. `pair_tiles`: rows 0 and 2 hold tile numbers; row 1 holds the neighbour code (0 to 13, see the steps) of the device that holds the second tile, or 14 for an empty slot; empty slots come after all listed entries. With code 0 the first tile is at most the second. Every pair of occupied tiles whose sub-boxes touch (faces, edges or corners, periodically) is listed exactly once, by the device for which the other device's offset is one of the 14 codes. At most 112 entries are listed on one device, and some device lists 112.
All inputs are finite; a program needn't handle non-finite values.
Results may differ from the reference program's by a relative error of at most 0.0003.
Values sent between devices are 32-bit elements; how exact they have to be, the bound alone decides.
A program may use at most 64 MiB of HBM per device.

```python
import math
import jax
import jax.numpy as jnp
import numpy as np
from jax import lax

TILE = 128
TILES = 8
SLOTS = 112
ITERS = 2
ATOMS = 1024
N_GX = 8
N_GY = 16
N_GZ = 4


SUB_EDGE = 10.85


shell_offsets = [(0, 0, 0), (0, 0, 1), (0, 1, -1), (0, 1, 0), (0, 1, 1), (1, -1, -1), (1, -1, 0), (1, -1, 1), (1, 0, -1), (1, 0, 0), (1, 0, 1), (1, 1, -1), (1, 1, 0), (1, 1, 1)]


def candidate_table():
    entries = []
    for near_code in range(14):
        offset = shell_offsets[near_code]
        for first_tile in range(8):
            for second_tile in range(8):
                first_cell = (first_tile // 4, first_tile // 2 % 2, first_tile % 2)
                second_cell = (second_tile // 4, second_tile // 2 % 2, second_tile % 2)
                if near_code == 0:
                    listed = first_tile <= second_tile
                else:
                    listed = all((abs(2 * offset[axis_number] + second_cell[axis_number] - first_cell[axis_number]) <= 1 for axis_number in range(3)))
                if listed:
                    entries.append((first_tile, near_code, second_tile))
    return np.array(entries, np.int32).T


def draw_positions(key, part):
    key = jax.random.fold_in(key, 7)
    layers = TILE // 16
    member = jnp.arange(TILE)
    lattice = jnp.stack([member // (4 * layers), member // layers % 4, member % layers]).astype(jnp.float32)
    spacing = jnp.array([SUB_EDGE / 4, SUB_EDGE / 4, SUB_EDGE / layers], jnp.float32)
    tile_number = jnp.arange(TILES)
    corner = jnp.stack([tile_number // 4, tile_number // 2 % 2, tile_number % 2]).astype(jnp.float32) * SUB_EDGE
    jitter = jax.random.uniform(key, (N_GX, N_GY, N_GZ, 3, TILES, TILE), jnp.float32, -0.25, 0.25)
    coords = corner[:, :, None] + (lattice[:, None, :] + 0.5 + jitter) * spacing[:, None, None]
    return coords.reshape(N_GX, N_GY, N_GZ, 3, TILES * TILE)


def draw_field(key, part):
    key = jax.random.fold_in(key, 9)
    base_key, spread_key = jax.random.split(key)
    shape = (N_GX, N_GY, N_GZ, 3, ATOMS)
    base = jnp.clip(jax.random.normal(base_key, shape, jnp.float32), -4.0, 4.0)
    spread = jnp.exp(jax.random.uniform(spread_key, (N_GX, N_GY, N_GZ, 1, ATOMS), jnp.float32, math.log(0.2), math.log(2.0)))
    level = jnp.arange(N_GZ).astype(jnp.float32)
    growth = 1.0 + 2.0 * level / (N_GZ - 1)
    return base * spread * growth[None, None, :, None, None]


def draw_pair_tiles(key, part):
    key = jax.random.fold_in(key, 5)
    table = jnp.asarray(candidate_table())
    slot_count = table.shape[1]
    level = jnp.arange(N_GZ)
    threshold = jnp.where(jnp.logical_or(level == 1, level == 2), 8, 1)
    rolled_dice = jax.random.randint(key, (N_GX, N_GY, N_GZ, TILES), 0, 8)
    occupied = rolled_dice < threshold[None, None, :, None]
    row_x = jnp.arange(N_GX)[:, None, None, None]
    row_y = jnp.arange(N_GY)[None, :, None, None]
    row_z = jnp.arange(N_GZ)[None, None, :, None]
    window = jnp.logical_and(jnp.logical_and(row_x <= 1, row_z == 0), jnp.logical_or(row_y <= 1, row_y == N_GY - 1))
    occupied = jnp.logical_or(occupied, window)
    shifted = jnp.stack([jnp.roll(occupied, (-ex, -ey, -ez), axis=(0, 1, 2)) for ex, ey, ez in shell_offsets])
    first_live = occupied[..., table[0]]
    second_live = jnp.transpose(shifted[table[1], :, :, :, table[2]], (1, 2, 3, 0))
    listed = jnp.logical_and(first_live, second_live)
    slot_index = jnp.arange(slot_count)
    order = jnp.argsort(jnp.where(listed, slot_index, slot_index + slot_count), axis=-1)
    ordered = jnp.transpose(jnp.take(table, order, axis=1), (1, 2, 3, 0, 4))
    kept = jnp.take_along_axis(listed, order, axis=-1)
    code_row = jnp.where(kept, ordered[..., 1, :], 14)
    return jnp.stack([ordered[..., 0, :], code_row, ordered[..., 2, :]], axis=3).astype(jnp.int32)


def block_levels(rng, dims, cuts, least, top_value):
    def one(axis_at, shards_of):
        steps = jax.random.uniform(jax.random.fold_in(jax.random.fold_in(rng, 6), axis_at), (shards_of,), jnp.float32, least / len(cuts), top_value / len(cuts))
        return jnp.repeat(jnp.exp(steps), dims[axis_at] // shards_of).reshape((-1,) + (1,) * (len(dims) - axis_at - 1))

    loudness = one(*cuts[0])
    for cut in cuts[1:]:
        loudness = loudness * one(*cut)
    return loudness


def length_profile(amount, total, bound, skew):
    weights = [(1 << 20) // math.isqrt(grade ** skew) + 1 for grade in range(2, amount + 1)]
    rest, given = total - bound - (amount - 1), [1] * (amount - 1)
    while rest > 0:
        movable = [i for i in range(amount - 1) if given[i] < bound]
        pool, remaining = sum([weights[i] for i in movable]), rest
        for i in movable:
            more = min(bound - given[i], max(1, remaining * weights[i] // pool), rest)
            given[i] = given[i] + more
            rest = rest - more
    return np.array([bound] + given)


def uneven_parts(stream_key, amount, total, limit, lean):
    if amount == 2:
        one = jax.random.randint(stream_key, (), max(1, total - limit), min(limit, total - 1) + 1)
        return jnp.stack([one, total - one])
    sizes = jnp.asarray(length_profile(amount, total, limit, lean), jnp.int32)
    couples = (amount - 1) // 2
    donor, taker = sizes[1:1 + 2 * couples:2], sizes[2:2 + 2 * couples:2]
    slack = jnp.minimum(donor - 1, limit - taker)
    passed = jax.random.randint(jax.random.fold_in(stream_key, 1), (couples,), 0, 1 << 20) % (slack + 1)
    sizes = sizes.at[1:1 + 2 * couples:2].set(donor - passed).at[2:2 + 2 * couples:2].set(taker + passed)
    return sizes[jax.random.permutation(jax.random.fold_in(stream_key, 2), amount)]


def setup_inputs(seed: int = 0) -> dict:
    splits = jax.random.split(jax.random.key(seed), 6)
    positions = draw_positions(jax.random.fold_in(splits[5], 71), 0)
    polar = jnp.clip(jnp.exp(math.log(3.0) - 2.014903 * jax.random.uniform(splits[1], (N_GX, N_GY, N_GZ, ATOMS), jnp.float32) ** block_levels(splits[1], (N_GX, N_GY, N_GZ, ATOMS), ((0, 8), (1, 16), (2, 4)), -0.2, 0.2)), 0.4, 3.0)
    field = draw_field(jax.random.fold_in(splits[5], 71), 0)
    groups = jax.vmap(lambda own: jnp.searchsorted(jnp.cumsum(uneven_parts(own, ATOMS // 4, ATOMS, 8, 0)), jnp.arange(ATOMS), side="right"))(jax.random.split(splits[3], N_GX * N_GY * N_GZ)).reshape((N_GX, N_GY, N_GZ, ATOMS)).astype(jnp.int32)
    pair_tiles = draw_pair_tiles(jax.random.fold_in(splits[5], 71), 0)
    return {"positions": positions, "polar": polar, "field": field, "groups": groups, "pair_tiles": pair_tiles}


THOLE_A = 0.39
BOX_EDGE = 21.7
CUT_ON = 7.0
CUT_OFF = 9.0
shell_offsets = [(0, 0, 0), (0, 0, 1), (0, 1, -1), (0, 1, 0), (0, 1, 1), (1, -1, -1), (1, -1, 0), (1, -1, 1), (1, 0, -1), (1, 0, 0), (1, 0, 1), (1, 1, -1), (1, 1, 0), (1, 1, 1)]

def coupling(first_pos, first_pol, second_pos, second_pol, offset, keep_mask):
    separation = second_pos[:, :, None, :] + offset[:, :, None, None] - first_pos[:, :, :, None]
    dist_sq = lax.optimization_barrier(jnp.sum(separation * separation, axis=0)) + jnp.where(keep_mask > 0, 0.0, 1.0)
    distance = jnp.sqrt(dist_sq)
    damping = (first_pol[:, :, None] * second_pol[:, None, :]) ** (1.0 / 6.0)
    damp_arg = THOLE_A * (distance / damping) ** 3
    screen_three = -jnp.expm1(-damp_arg)
    screen_five = screen_three - damp_arg * jnp.exp(-damp_arg)
    switch_arg = jnp.clip((distance - CUT_ON) / (CUT_OFF - CUT_ON), 0.0, 1.0)
    switch_val = 1.0 - switch_arg ** 3 * (10.0 - 15.0 * switch_arg + 6.0 * switch_arg * switch_arg)
    inv_cube = keep_mask * switch_val / (dist_sq * distance)
    return (separation, screen_three * inv_cube, 3.0 * screen_five * inv_cube / dist_sq)

def field_first(separation, coef_three, coef_five, second_dip):
    along = lax.optimization_barrier(jnp.sum(separation * second_dip[:, :, None, :], axis=0))
    return lax.optimization_barrier(jnp.sum(coef_five * along * separation - coef_three * second_dip[:, :, None, :], axis=-1))

def field_second(separation, coef_three, coef_five, first_dip):
    along = lax.optimization_barrier(jnp.sum(separation * first_dip[:, :, :, None], axis=0))
    return lax.optimization_barrier(jnp.sum(coef_five * along * separation - coef_three * first_dip[:, :, :, None], axis=-2))

def pair_keep(first_tile, near_code, second_tile, group_tile):
    listed = near_code < 14
    same_device = near_code == 0
    differ = group_tile[first_tile][:, :, None] != group_tile[second_tile][:, None, :]
    allowed = jnp.logical_and(listed[:, None, None], jnp.logical_or(jnp.logical_not(same_device)[:, None, None], differ))
    weight = jnp.where(jnp.logical_and(same_device, first_tile == second_tile), 0.5, 1.0)
    return allowed.astype(jnp.float32) * weight[:, None, None]

def pair_offsets(near_code):
    clamped = jnp.minimum(near_code, 13)
    table = jnp.array(shell_offsets, jnp.float32).T
    return BOX_EDGE * table[:, clamped]

def reference(positions, polar, field, groups, pair_tiles):
    grid_shape = positions.shape[:3]
    device_count = N_GX * N_GY * N_GZ
    atom_data = jnp.concatenate([positions, polar[:, :, :, None, :]], axis=3)

    def neighbours(array):
        rolled = [jnp.roll(array, (-ex, -ey, -ez), axis=(0, 1, 2)) for ex, ey, ez in shell_offsets]
        return jnp.stack(rolled).reshape(14, device_count, array.shape[3], TILES, TILE)
    own_atoms = atom_data.reshape(device_count, 4, TILES, TILE)
    near_atoms = neighbours(atom_data)
    group_tiles = groups.reshape(device_count, TILES, TILE)
    pair_lists = pair_tiles.reshape(device_count, 3, SLOTS)

    def apply_coupling(dipole_field):
        own_dip = dipole_field.reshape(device_count, 3, TILES, TILE)
        near_dip = neighbours(dipole_field)

        def per_device(device_index):
            entries = pair_lists[device_index]
            first_tile, near_code, second_tile = (entries[0], entries[1], entries[2])
            clamped = jnp.minimum(near_code, 13)
            own_data = own_atoms[device_index]
            second_data = jnp.transpose(near_atoms[:, device_index][clamped, :, second_tile], (1, 0, 2))
            keep_mask = pair_keep(first_tile, near_code, second_tile, group_tiles[device_index])
            separation, coef_three, coef_five = coupling(own_data[:3][:, first_tile], own_data[3][first_tile], second_data[:3], second_data[3], pair_offsets(near_code), keep_mask)
            first_dip = own_dip[device_index][:, first_tile]
            second_dip = jnp.transpose(near_dip[:, device_index][clamped, :, second_tile], (1, 0, 2))
            on_first = field_first(separation, coef_three, coef_five, second_dip)
            on_second = field_second(separation, coef_three, coef_five, first_dip)
            own_field = jnp.zeros((3, TILES, TILE), jnp.float32).at[:, first_tile].add(on_first)
            far_field = jnp.zeros((14, 3, TILES, TILE), jnp.float32).at[clamped, :, second_tile].add(jnp.transpose(on_second, (1, 0, 2)))
            return (own_field, far_field)
        own_field, far_field = lax.map(per_device, jnp.arange(device_count))
        total = own_field.reshape(grid_shape + (3, ATOMS))
        far_field = far_field.reshape(grid_shape + (14, 3, ATOMS))
        for near_code in range(14):
            ex, ey, ez = shell_offsets[near_code]
            total = total + jnp.roll(far_field[:, :, :, near_code], (ex, ey, ez), axis=(0, 1, 2))
        return total
    polar_all = polar[:, :, :, None, :]
    dipoles = polar_all * field
    residual = apply_coupling(dipoles)
    precond = polar_all * residual
    search = precond
    precond_dot = jnp.sum(residual * precond)
    for iteration in range(ITERS):
        applied = search / polar_all - apply_coupling(search)
        descent = precond_dot / jnp.sum(search * applied)
        dipoles = dipoles + descent * search
        residual = residual - descent * applied
        if iteration + 1 < ITERS:
            precond = polar_all * residual
            next_dot = jnp.sum(residual * precond)
            search = precond + next_dot / precond_dot * search
            precond_dot = next_dot
    return (dipoles, residual)
```

```python
import functools

import jax
import jax.numpy as jnp
import numpy as np
from jax import lax
from jax.experimental import pallas as pl
from jax.experimental.pallas import tpu as pltpu
from jax.sharding import PartitionSpec as P

TILE = 128
TILES = 8
AXES = ("gx", "gy", "gz")
BOX_EDGE = 21.7
THOLE_A = 0.39
FAR = 1000.0
MESH = pl.DeviceIdType.MESH
SHELL = [
    (0, 0, 0), (0, 0, 1), (0, 1, -1), (0, 1, 0), (0, 1, 1), (1, -1, -1), (1, -1, 0),
    (1, -1, 1), (1, 0, -1), (1, 0, 0), (1, 0, 1), (1, 1, -1), (1, 1, 0), (1, 1, 1),
]
N_SLOTS = 28
FACE, EDGE, CORNER, OWN, SELF = 0, 48, 72, 76, 104
ENTRIES = 112


def face_first(f, p):
    s = 1 + f + f * (f - 1) // 2
    return p // s * (2 * s) + s + p % s


def edge_first(k, p):
    g, sg = k // 2, k % 2
    free = 4 - 2 * g + g * (g - 1) // 2
    return free * p + 4 - 2 * ((2 - g) // 2) + (1 + g // 2) * sg


def corner_first(k):
    return 4 + k


def tables():
    messages, slot_tile, keys = [], [], []
    for f in range(3):
        s = 1 << f
        e = [0, 0, 0]
        e[2 - f] = 1
        messages.append((tuple(e), len(slot_tile), 4))
        slot_tile += [q // s * 2 * s + q % s for q in range(4)]
    for k in range(6):
        g, sg = k // 2, k % 2
        e = [[0, 1, 2 * sg - 1], [1, 0, 2 * sg - 1], [1, 2 * sg - 1, 0]][g]
        free, low = (4, 2, 1)[g], (1, 1, 2)[g]
        messages.append((tuple(e), len(slot_tile), 2))
        slot_tile += [free * q + low * (1 - sg) for q in range(2)]
    for k in range(4):
        sy, sz = k // 2, k % 2
        messages.append(((1, 2 * sy - 1, 2 * sz - 1), len(slot_tile), 1))
        slot_tile += [2 * (1 - sy) + 1 - sz]
    for m, (e, start, count) in enumerate(messages):
        for slot in range(start, start + count):
            for p in range(count):
                if m < 3:
                    a = face_first(m, p)
                elif m < 9:
                    a = edge_first(m - 3, p)
                else:
                    a = corner_first(m - 9)
                keys.append((a, SHELL.index(e), slot_tile[slot]))
    for n in range(28):
        a, b = n % 8, (n % 8 + n // 8 + 1) % 8
        keys.append((min(a, b), 0, max(a, b)))
    keys += [(a, 0, a) for a in range(8)]
    assert len(set(keys)) == ENTRIES
    key = np.array([a * 128 + c * 8 + b for a, c, b in keys], np.int32)
    return messages, slot_tile, np.ascontiguousarray(np.broadcast_to(key[:, None], (ENTRIES, 128)))


MESSAGES, SLOT_TILE, KEYS = tables()
N_MSG = len(MESSAGES)


def halves(tile):
    hi = tile.astype(jnp.bfloat16).astype(jnp.float32)
    return hi, (tile - hi)


def two_parts(tile):
    hi, rest = halves(tile)
    return jnp.concatenate([hi, rest], axis=0).astype(jnp.bfloat16)


def three_parts(tile):
    hi, rest = halves(tile)
    mid, low = halves(rest)
    return jnp.concatenate([hi, mid, low, jnp.zeros_like(low)], axis=0)


def fold_parts(parts):
    both = parts[0:8] + parts[8:16]
    if both.shape[1] == 256:
        both = both[:, :128] + both[:, 128:]
    return both


def kernel(sizes, pos, pol, fld, grp, prs, keys, dip_out, res_out,
           hxyz, c3p, xi, mi, ms, f1, g1, f2own, g2own, flag, xj,
           own, vec, polar8, send, halo, back, fold, ar_send, ar_recv,
           hs_sem, hr_sem, fs_sem, fr_sem, as_sem, ar_sem):
    f32, bf16 = jnp.float32, jnp.bfloat16
    nx, ny, nz = sizes
    me = tuple(lax.axis_index(a) for a in AXES)
    gx, gy, gz = me

    def at(e):
        return tuple(lax.rem(m + d + n, n) for m, d, n in zip(me, e, sizes))

    core, zed = lax.rem(gy, 2), gy // 2

    def partner(phase, k):
        if phase == 0:
            j = lax.rem(core * 4 + gz + k, 8)
            return (gx, gy - core + j // 4, lax.rem(j, 4))
        if phase == 1:
            return (lax.rem(gx + k, 8), gy, gz)
        return (gx, lax.rem(zed + k, 8) * 2 + core, gz)

    barrier = pltpu.get_barrier_semaphore()
    signals = 0
    for e, _, _ in MESSAGES:
        for sign in (1, -1):
            pl.semaphore_signal(barrier, inc=1, device_id=at(tuple(sign * d for d in e)), device_id_type=MESH)
            signals += 1
    for phase in range(3):
        for k in range(1, 8):
            pl.semaphore_signal(barrier, inc=1, device_id=partner(phase, k), device_id_type=MESH)
            signals += 1

    row = lax.broadcasted_iota(jnp.int32, (8, 128), 0)
    vec_rows = jnp.logical_and(row >= 4, row < 7)

    def put(x, y, z):
        return jnp.where(row == 4, x, jnp.where(row == 5, y, jnp.where(row == 6, z, 0.0)))

    for a in range(TILES):
        cols = slice(a * TILE, (a + 1) * TILE)
        p = pol[:, cols]
        polar8[a] = jnp.broadcast_to(p, (8, 128))
        own[0, a] = jnp.concatenate(
            [pos[:, cols], lax.rsqrt(p), p * fld[:, cols], grp[:, cols].astype(f32)], axis=0
        )

    def halo_copy(r, m):
        e, start, count = MESSAGES[m]
        return pltpu.make_async_remote_copy(
            src_ref=send.at[r, pl.ds(start, count)], dst_ref=halo.at[r, pl.ds(start, count)],
            send_sem=hs_sem.at[r, m], recv_sem=hr_sem.at[r, m],
            device_id=at(tuple(-d for d in e)), device_id_type=MESH)

    def fold_copy(r, m):
        e, start, count = MESSAGES[m]
        return pltpu.make_async_remote_copy(
            src_ref=back.at[r, pl.ds(start, count)], dst_ref=fold.at[r, pl.ds(start, count)],
            send_sem=fs_sem.at[r, m], recv_sem=fr_sem.at[r, m],
            device_id=at(e), device_id_type=MESH)

    def send_halo(r):
        for slot in range(N_SLOTS):
            send[r, slot] = own[r, SLOT_TILE[slot]]
        for m in range(N_MSG):
            halo_copy(r, m).start()

    for slot in range(N_SLOTS):
        send[0, slot] = own[0, SLOT_TILE[slot]]
    pl.semaphore_wait(barrier, signals)
    for m in range(N_MSG):
        halo_copy(0, m).start()

    key_row = prs[0:1] * 128 + prs[1:2] * 8 + prs[2:3]
    hit = jnp.where(keys[:, : key_row.shape[1]] == key_row, 0.0, FAR)
    flag[...] = jnp.broadcast_to(jnp.min(hit, axis=1, keepdims=True), (ENTRIES, 128))

    def spread(width, first):
        k = lax.broadcasted_iota(jnp.int32, (32, width * 128), 0)
        c = lax.broadcasted_iota(jnp.int32, (32, width * 128), 1) // 128
        return jnp.where(jnp.logical_and(k % 8 == c + first, k < 24), 1.0, 0.0).astype(bf16)

    spread_all = spread(8, 0)
    spread_vec = spread(3, 4)

    def broadcast_own(a, carry):
        cols = jnp.transpose(three_parts(own[0, a])).astype(bf16)
        wide = jnp.dot(cols, spread_all, preferred_element_type=f32)
        xi[a, :, 0:384] = wide[:, 0:384]
        xi[a, :, 384:512] = wide[:, 384:512] * -THOLE_A
        xi[a, :, 512:640] = wide[:, 896:1024]
        mi[a] = wide[:, 512:896]
        parts = two_parts(own[0, a])
        ms[a] = jnp.concatenate([parts, parts], axis=1)
        return carry

    def broadcast_vec(r):
        def one(a, carry):
            cols = jnp.transpose(three_parts(own[r, a])).astype(bf16)
            mi[a] = jnp.dot(cols, spread_vec, preferred_element_type=f32)
            parts = two_parts(own[r, a])
            ms[a] = jnp.concatenate([parts, parts], axis=1)
            return carry

        lax.fori_loop(0, TILES, one, 0)

    lax.fori_loop(0, TILES, broadcast_own, 0)

    def coefficients(n, a, tile, grouped):
        shift = flag[pl.ds(n, 1), :]
        xs = [jnp.broadcast_to(tile[c : c + 1], (16, 128)) for c in range(4)]
        xs[0] = xs[0] + jnp.broadcast_to(shift, (16, 128))
        group = jnp.broadcast_to(tile[7:8], (16, 128))
        for g in range(8):
            rows = slice(16 * g, 16 * g + 16)
            s = [xs[c] - xi[a, rows, c * 128 : c * 128 + 128] for c in range(3)]
            r2 = s[0] * s[0] + s[1] * s[1] + s[2] * s[2]
            if grouped:
                r2 = jnp.where(xi[a, rows, 512:640] == group, FAR * FAR, r2)
            rinv = lax.rsqrt(r2)
            r = r2 * rinv
            x = r2 * r * (xi[a, rows, 384:512] * xs[3])
            ex = jnp.exp(x)
            l3 = 1.0 - ex
            l5 = l3 + x * ex
            v = jnp.clip(r - 8.0, -1.0, 1.0)
            v2 = v * v
            cut = jnp.maximum(0.5 - v * ((v2 * 0.1875 - 0.625) * v2 + 0.9375), 0.0)
            rinv2 = rinv * rinv
            w = cut * (rinv2 * rinv)
            c3 = w * l3
            c5 = (w * 3.0) * rinv2 * l5
            q = c5 * lax.rsqrt(jnp.maximum(c5, 1e-36))
            for c in range(3):
                hxyz[n, c, rows, :] = q * s[c]
            hi = c3.astype(bf16)
            c3p[n, rows, :] = hi
            c3p[n, 128 + 16 * g : 144 + 16 * g, :] = (c3 - hi.astype(f32)).astype(bf16)

    def apply(entries, tile, both=True, first=False):
        mj = [jnp.broadcast_to(tile[4 + c : 5 + c], (8, 128)) for c in range(3)]
        mj_parts = two_parts(tile)
        on_second, c3_second = None, None
        for n, a in entries:
            one = lax.dot_general(mj_parts, c3p[n], (((1,), (1,)), ((), ())), preferred_element_type=f32)
            g1[a] = one if first else g1[a] + one
            if both:
                two = jnp.dot(ms[a], c3p[n], preferred_element_type=f32)
                c3_second = two if c3_second is None else c3_second + two
        for n, a in entries:
            for g in range(16):
                rows = slice(8 * g, 8 * g + 8)
                h = [hxyz[n, c, rows, :] for c in range(3)]
                dj = h[0] * mj[0] + h[1] * mj[1] + h[2] * mj[2]
                for c in range(3):
                    if first:
                        f1[a, c, rows, :] = h[c] * dj
                    else:
                        f1[a, c, rows, :] += h[c] * dj
                if both:
                    m = [mi[a, rows, c * 128 : c * 128 + 128] for c in range(3)]
                    di = h[0] * m[0] + h[1] * m[1] + h[2] * m[2]
                    if on_second is None:
                        on_second = [h[c] * di for c in range(3)]
                    else:
                        on_second = [on_second[c] + h[c] * di for c in range(3)]
        return on_second, c3_second

    def own_pairs(r, low, high):
        def one(k, carry):
            for u in range(4):
                n = k * 4 + u
                a = n % 8
                b = (a + n // 8 + 1) % 8
                tile = own[r, b]
                if r == 0:
                    coefficients(OWN + n, a, tile, True)
                fields, c3_fields = apply([(OWN + n, a)], tile)
                for c in range(3):
                    f2own[b, c] += fields[c]
                g2own[b] += c3_fields
            return carry

        lax.fori_loop(low, high, one, 0)

    def selves(r):
        def one(k, carry):
            for u in range(2):
                a = k * 2 + u
                tile = own[r, a]
                if r == 0:
                    coefficients(SELF + a, a, tile, True)
                apply([(SELF + a, a)], tile, both=False, first=True)
            return carry

        lax.fori_loop(0, 4, one, 0)

    def halo_tiles(r, low, high, entries_of):
        def one(slot, carry):
            entries = entries_of(slot)
            tile = halo[r, slot]
            if r == 0:
                for n, a in entries:
                    coefficients(n, a, xj[slot], False)
            fields, c3_fields = apply(entries, tile)
            back[r, slot] = put(*[jnp.sum(f, axis=0, keepdims=True) for f in fields]) - jnp.where(
                vec_rows, fold_parts(c3_fields), 0.0)
            return carry

        lax.fori_loop(low, high, one, 0)

    def face_entries(slot):
        return [(FACE + slot * 4 + p, face_first(slot // 4, p)) for p in range(4)]

    def edge_entries(slot):
        k = slot - 12
        return [(EDGE + k * 2 + p, edge_first(k // 2, p)) for p in range(2)]

    def corner_entries(slot):
        return [(CORNER + slot - 24, corner_first(slot - 24))]

    ones = jnp.ones((8, 128), f32)

    def run_round(r):
        selves(r)
        own_pairs(r, 0, 4)
        for m in range(N_MSG):
            halo_copy(r, m).wait_recv()
        if r == 0:
            for e, start, count in MESSAGES:
                shift = jnp.where(row == 0, e[0] * BOX_EDGE, 0.0) + jnp.where(
                    row == 1, e[1] * BOX_EDGE, 0.0) + jnp.where(row == 2, e[2] * BOX_EDGE, 0.0)
                for slot in range(start, start + count):
                    xj[slot] = halo[0, slot] + shift
        halo_tiles(r, 0, 12, face_entries)
        for m in range(3):
            fold_copy(r, m).start()
        halo_tiles(r, 12, 24, edge_entries)
        for m in range(3, 9):
            fold_copy(r, m).start()
        halo_tiles(r, 24, 28, corner_entries)
        for m in range(9, 13):
            fold_copy(r, m).start()
        own_pairs(r, 4, 7)

        def gather_own(a, carry):
            lanes = lax.dot_general(
                ones, f1[a].reshape(384, 128), (((1,), (1,)), ((), ())),
                precision=lax.Precision.HIGHEST, preferred_element_type=f32)
            total = put(*[
                lanes[:, c * 128 : c * 128 + 128] + jnp.sum(f2own[a, c], axis=0, keepdims=True)
                for c in range(3)])
            vec[r, a] = total - jnp.where(vec_rows, fold_parts(g1[a]) + fold_parts(g2own[a]), 0.0)
            return carry

        lax.fori_loop(0, TILES, gather_own, 0)

    def add_folded(r):
        for m in range(N_MSG):
            fold_copy(r, m).wait_recv()
        for slot in range(N_SLOTS):
            vec[r, SLOT_TILE[slot]] += fold[r, slot]

    def clear():
        f2own[...] = jnp.zeros_like(f2own)
        g2own[...] = jnp.zeros_like(g2own)

    def rows_dot(left, right):
        total = left(0) * right(0)
        for a in range(1, TILES):
            total = total + left(a) * right(a)
        return total

    for r in range(3):
        if r > 0:
            broadcast_vec(r)
        clear()
        run_round(r)
        if r < 2:
            add_folded(r)
            for a in range(TILES):
                own[r + 1, a] = polar8[a] * vec[r, a]
            send_halo(r + 1)

    g00 = rows_dot(lambda a: vec[0, a], lambda a: own[1, a])
    g01 = rows_dot(lambda a: vec[1, a], lambda a: own[1, a])
    g11 = rows_dot(lambda a: vec[1, a], lambda a: own[2, a])
    g12 = rows_dot(lambda a: vec[2, a], lambda a: own[2, a])
    for slot in range(N_SLOTS):
        g12 = g12 + halo[2, slot] * back[2, slot]

    def phase_copy(phase, k):
        return pltpu.make_async_remote_copy(
            src_ref=ar_send.at[phase], dst_ref=ar_recv.at[phase, k - 1],
            send_sem=as_sem.at[phase, k - 1], recv_sem=ar_sem.at[phase, k - 1],
            device_id=partner(phase, k), device_id_type=MESH)

    parts = [jnp.sum(g, axis=0, keepdims=True) for g in (g00, g01, g11, g12)]
    total = jnp.where(row == 0, parts[0], jnp.where(row == 1, parts[1], jnp.where(row == 2, parts[2], parts[3])))
    for phase in range(3):
        ar_send[phase] = total
        for k in range(1, 8):
            phase_copy(phase, k).start()
        if phase == 0:
            add_folded(2)
        for k in range(1, 8):
            phase_copy(phase, k).wait_recv()
            total = total + ar_recv[phase, k - 1]

    sums = jnp.sum(total, axis=1, keepdims=True)
    s00, s01, s11, s12 = (sums[i : i + 1] for i in range(4))
    alpha = s00 / (s00 - s01)
    keep = 1.0 - alpha
    rho = keep * keep * s00 + 2.0 * keep * alpha * s01 + alpha * alpha * s11
    a0 = keep + rho / s00
    a1 = alpha
    denom = (a0 * a0 * s00 + 2.0 * a0 * a1 * s01 + a1 * a1 * s11) - (
        a0 * a0 * s01 + 2.0 * a0 * a1 * s11 + a1 * a1 * s12)
    step = rho / denom
    d1, d2 = alpha + step * a0, step * a1
    r0, r1, r2 = keep - step * a0, alpha - step * a1 + step * a0, step * a1
    for a in range(TILES):
        cols = slice(a * TILE, (a + 1) * TILE)
        dip = own[0, a] + d1 * own[1, a] + d2 * own[2, a]
        res = r0 * vec[0, a] + r1 * vec[1, a] + r2 * vec[2, a]
        dip_out[:, cols] = dip[4:7]
        res_out[:, cols] = res[4:7]

    for r in range(3):
        for m in range(N_MSG):
            halo_copy(r, m).wait_send()
            fold_copy(r, m).wait_send()
    for phase in range(3):
        for k in range(1, 8):
            phase_copy(phase, k).wait_send()


def solution(mesh):
    sizes = tuple(mesh.shape[a] for a in AXES)
    f32, bf16 = jnp.float32, jnp.bfloat16

    def shards(positions, polar, field, groups, pair_tiles):
        vmem = pl.BlockSpec(memory_space=pltpu.VMEM)
        dma = pltpu.SemaphoreType.DMA
        scratch = [
            pltpu.VMEM((ENTRIES, 3, 128, 128), f32),
            pltpu.VMEM((ENTRIES, 256, 128), bf16),
            pltpu.VMEM((8, 128, 640), f32),
            pltpu.VMEM((8, 128, 384), f32),
            pltpu.VMEM((8, 16, 256), bf16),
            pltpu.VMEM((8, 3, 128, 128), f32),
            pltpu.VMEM((8, 16, 256), f32),
            pltpu.VMEM((8, 3, 8, 128), f32),
            pltpu.VMEM((8, 16, 128), f32),
            pltpu.VMEM((ENTRIES, 128), f32),
            pltpu.VMEM((N_SLOTS, 8, 128), f32),
            pltpu.VMEM((3, 8, 8, 128), f32),
            pltpu.VMEM((3, 8, 8, 128), f32),
            pltpu.VMEM((8, 8, 128), f32),
            pltpu.VMEM((3, N_SLOTS, 8, 128), f32),
            pltpu.VMEM((3, N_SLOTS, 8, 128), f32),
            pltpu.VMEM((3, N_SLOTS, 8, 128), f32),
            pltpu.VMEM((3, N_SLOTS, 8, 128), f32),
            pltpu.VMEM((3, 8, 128), f32),
            pltpu.VMEM((3, 7, 8, 128), f32),
            dma((3, N_MSG)), dma((3, N_MSG)), dma((3, N_MSG)), dma((3, N_MSG)),
            dma((3, 7)), dma((3, 7)),
        ]
        atoms = positions.shape[-1]
        out = jax.ShapeDtypeStruct((3, atoms), f32)
        dip, res = pl.pallas_call(
            functools.partial(kernel, sizes),
            out_shape=(out, out),
            in_specs=[vmem] * 6,
            out_specs=(vmem, vmem),
            scratch_shapes=scratch,
            compiler_params=pltpu.CompilerParams(
                collective_id=0, has_side_effects=True, vmem_limit_bytes=50 * 1024 * 1024),
            name="dipole_cg",
        )(positions.reshape(3, atoms), polar.reshape(1, atoms), field.reshape(3, atoms),
          groups.reshape(1, atoms), pair_tiles.reshape(3, -1), jnp.asarray(KEYS))
        return dip.reshape(1, 1, 1, 3, atoms), res.reshape(1, 1, 1, 3, atoms)

    placed = (
        P(*AXES, None, None), P(*AXES, None), P(*AXES, None, None), P(*AXES, None), P(*AXES, None, None))
    return jax.shard_map(
        shards, mesh=mesh, in_specs=placed, out_specs=(placed[0], placed[0]), check_vma=False)
```

```python
import functools

import jax
import jax.numpy as jnp
import numpy as np
from jax import lax
from jax.experimental import pallas as pl
from jax.experimental.pallas import tpu as pltpu
from jax.sharding import PartitionSpec as P

TILE = 128
TILES = 8
AXES = ("gx", "gy", "gz")
BOX_EDGE = 21.7
THOLE_A = 0.39
FAR = 1000.0
SCALE = 3.0 / 16.0
C10 = np.float32(10.0 / 3.0)
C8 = np.float32(5.0) - (C10 - np.float32(1.0))
MESH = pl.DeviceIdType.MESH
SHELL = [
    (0, 0, 0), (0, 0, 1), (0, 1, -1), (0, 1, 0), (0, 1, 1), (1, -1, -1), (1, -1, 0),
    (1, -1, 1), (1, 0, -1), (1, 0, 0), (1, 0, 1), (1, 1, -1), (1, 1, 0), (1, 1, 1),
]
N_SLOTS = 28
FACE, EDGE, CORNER, OWN, LAST = 0, 48, 72, 76, 108
ENTRIES = 112


def face_first(f, p):
    s = 1 + f + f * (f - 1) // 2
    return p // s * (2 * s) + s + p % s


def edge_first(k, p):
    g, sg = k // 2, k % 2
    free = 4 - 2 * g + g * (g - 1) // 2
    return free * p + 4 - 2 * ((2 - g) // 2) + (1 + g // 2) * sg


def corner_first(k):
    return 4 + k


def tables():
    messages, slot_tile, keys = [], [], []
    for f in range(3):
        s = 1 << f
        e = [0, 0, 0]
        e[2 - f] = 1
        messages.append((tuple(e), len(slot_tile), 4))
        slot_tile += [q // s * 2 * s + q % s for q in range(4)]
    for k in range(6):
        g, sg = k // 2, k % 2
        e = [[0, 1, 2 * sg - 1], [1, 0, 2 * sg - 1], [1, 2 * sg - 1, 0]][g]
        free, low = (4, 2, 1)[g], (1, 1, 2)[g]
        messages.append((tuple(e), len(slot_tile), 2))
        slot_tile += [free * q + low * (1 - sg) for q in range(2)]
    for k in range(4):
        sy, sz = k // 2, k % 2
        messages.append(((1, 2 * sy - 1, 2 * sz - 1), len(slot_tile), 1))
        slot_tile += [2 * (1 - sy) + 1 - sz]
    for m, (e, start, count) in enumerate(messages):
        for p in range(count):
            if m < 3:
                a = face_first(m, p)
            elif m < 9:
                a = edge_first(m - 3, p)
            else:
                a = corner_first(m - 9)
            keys += [(a, SHELL.index(e), slot_tile[start + q]) for q in range(count)]
    for a in range(8):
        for d in range(4):
            b = (a + d) % 8
            keys.append((min(a, b), 0, max(a, b)))
    keys += [(a, 0, a + 4) for a in range(4)]
    assert len(set(keys)) == ENTRIES
    key = np.array([a * 128 + c * 8 + b for a, c, b in keys], np.int32)
    return messages, slot_tile, np.ascontiguousarray(np.broadcast_to(key[:, None], (ENTRIES, 128)))


MESSAGES, SLOT_TILE, KEYS = tables()
N_MSG = len(MESSAGES)


def halves(tile):
    hi = tile.astype(jnp.bfloat16).astype(jnp.float32)
    return hi, (tile - hi)


def two_parts(tile):
    hi, rest = halves(tile)
    return jnp.concatenate([hi, rest], axis=0).astype(jnp.bfloat16)


def fold_parts(parts):
    return parts[0:8] + parts[8:16]


def kernel(sizes, pos, pol, fld, grp, prs, keys, dip_out, res_out,
           hxyz, c3p, xi, mi, ms, mjp, f1, g1, f2own, g2own, flag, xj,
           own, vec, polar8, send, halo, back, fold, ar_send, ar_recv,
           hs_sem, hr_sem, fs_sem, fr_sem, as_sem, ar_sem):
    f32, bf16 = jnp.float32, jnp.bfloat16
    me = tuple(lax.axis_index(a) for a in AXES)
    gx, gy, gz = me

    def at(e):
        return tuple(lax.rem(m + d + n, n) for m, d, n in zip(me, e, sizes))

    core, zed = lax.rem(gy, 2), gy // 2

    def partner(phase, k):
        if phase == 0:
            j = lax.rem(core * 4 + gz + k, 8)
            return (gx, gy - core + j // 4, lax.rem(j, 4))
        if phase == 1:
            return (lax.rem(gx + k, 8), gy, gz)
        return (gx, lax.rem(zed + k, 8) * 2 + core, gz)

    barrier = pltpu.get_barrier_semaphore()
    signals = 0
    for e, _, _ in MESSAGES:
        for sign in (1, -1):
            pl.semaphore_signal(barrier, inc=1, device_id=at(tuple(sign * d for d in e)), device_id_type=MESH)
            signals += 1
    for phase in range(3):
        for k in range(1, 8):
            pl.semaphore_signal(barrier, inc=1, device_id=partner(phase, k), device_id_type=MESH)
            signals += 1

    row = lax.broadcasted_iota(jnp.int32, (8, 128), 0)
    vec_rows = jnp.logical_and(row >= 4, row < 7)

    def put(x, y, z):
        return jnp.where(row == 4, x, jnp.where(row == 5, y, jnp.where(row == 6, z, 0.0)))

    def tile_field(sums, parts):
        rows = [jnp.sum(f, axis=0, keepdims=True) for f in sums]
        return put(*rows) - jnp.where(vec_rows, fold_parts(parts), 0.0)

    for a in range(TILES):
        p = pol[a : a + 1]
        polar8[a] = jnp.broadcast_to(p * SCALE, (8, 128))
        own[0, a] = jnp.concatenate(
            [pos[8 * c + a : 8 * c + a + 1] for c in range(3)] + [lax.rsqrt(p)]
            + [p * SCALE * fld[8 * c + a : 8 * c + a + 1] for c in range(3)]
            + [grp[a : a + 1].astype(f32)], axis=0)

    def halo_copy(r, m):
        e, start, count = MESSAGES[m]
        return pltpu.make_async_remote_copy(
            src_ref=send.at[r, pl.ds(start, count)], dst_ref=halo.at[r, pl.ds(start, count)],
            send_sem=hs_sem.at[r, m], recv_sem=hr_sem.at[r, m],
            device_id=at(tuple(-d for d in e)), device_id_type=MESH)

    def fold_copy(r, m):
        e, start, count = MESSAGES[m]
        return pltpu.make_async_remote_copy(
            src_ref=back.at[r, pl.ds(start, count)], dst_ref=fold.at[r, pl.ds(start, count)],
            send_sem=fs_sem.at[r, m], recv_sem=fr_sem.at[r, m],
            device_id=at(e), device_id_type=MESH)

    def send_halo(r):
        for slot in range(N_SLOTS):
            send[r, slot] = own[r, SLOT_TILE[slot]]
        if r == 0:
            pl.semaphore_wait(barrier, signals)
        for m in range(N_MSG):
            halo_copy(r, m).start()

    send_halo(0)

    key_row = prs[0] * 128 + prs[1] * 8 + prs[2]
    hit = jnp.where(keys[:, : key_row.shape[1]] == key_row, 0.0, FAR)
    flag[...] = jnp.broadcast_to(jnp.min(hit, axis=1, keepdims=True), (ENTRIES, 128))

    def columns(r):
        cols = jnp.transpose(own[r].reshape(64, 128))
        for a in range(TILES):
            def wide(k, scale):
                return jnp.broadcast_to(cols[:, a * 8 + k : a * 8 + k + 1] * scale, (128, 128))

            for c in range(3):
                mi[a, :, c * 128 : c * 128 + 128] = wide(4 + c, 3.0)
            if r == 0:
                for c in range(3):
                    xi[a, :, c * 128 : c * 128 + 128] = wide(c, 1.0)
                xi[a, :, 384:512] = wide(3, -THOLE_A)
                xi[a, :, 512:640] = wide(7, 1.0)
            parts = two_parts(own[r, a])
            ms[a] = jnp.concatenate([parts, parts], axis=1)

    def coefficients(n, a, tile, grouped):
        shift = flag[pl.ds(n, 1), :]
        xs = [jnp.broadcast_to(tile[c : c + 1], (16, 128)) for c in range(4)]
        xs[0] = xs[0] + jnp.broadcast_to(shift, (16, 128))
        group = jnp.broadcast_to(tile[7:8], (16, 128))
        for g in range(8):
            rows = slice(16 * g, 16 * g + 16)
            s = [xs[c] - xi[a, rows, c * 128 : c * 128 + 128] for c in range(3)]
            r2 = s[0] * s[0] + s[1] * s[1] + s[2] * s[2]
            if grouped:
                r2 = jnp.where(xi[a, rows, 512:640] == group, FAR * FAR, r2)
            rinv = lax.rsqrt(r2)
            r = r2 * rinv
            x = r2 * r * (xi[a, rows, 384:512] * xs[3])
            ex = jnp.exp(x)
            l3 = 1.0 - ex
            v = jnp.clip(r - 8.0, -1.0, 1.0)
            v2 = v * v
            cut = jnp.maximum(C8 - v * ((v2 - C10) * v2 + 5.0), 0.0)
            w = cut * (rinv * rinv * rinv)
            c3 = w * l3
            q2 = w * (l3 + x * ex)
            q = q2 * lax.rsqrt(jnp.maximum(q2, 1e-36)) * rinv
            for c in range(3):
                hxyz[n, c, rows, :] = q * s[c]
            hi = c3.astype(bf16)
            c3p[n, rows, :] = hi
            c3p[n, 128 + 16 * g : 144 + 16 * g, :] = (c3 - hi.astype(f32)).astype(bf16)

    def beside(ns):
        return jnp.concatenate([c3p[n] for n in ns], axis=1) if len(ns) > 1 else c3p[ns[0]]

    def dot_rows(h, m):
        return h[0] * m[0] + h[1] * m[1] + h[2] * m[2]

    def on_seconds(firsts):
        count = len(firsts[0][1])
        sums, parts = [None] * count, None
        for a, ns in firsts:
            part = jnp.dot(ms[a], beside(ns), preferred_element_type=f32)
            parts = part if parts is None else parts + part
        for a, ns in firsts:
            for g in range(16):
                rows = slice(8 * g, 8 * g + 8)
                m = [mi[a, rows, c * 128 : c * 128 + 128] for c in range(3)]
                for q in range(count):
                    h = [hxyz[ns[q], c, rows, :] for c in range(3)]
                    d = dot_rows(h, m)
                    add = [h[c] * d for c in range(3)]
                    sums[q] = add if sums[q] is None else [sums[q][c] + add[c] for c in range(3)]
        return [(sums[q], parts[:, q * 128 : q * 128 + 128]) for q in range(count)]

    def triple(tile):
        return [jnp.broadcast_to(tile[4 + c : 5 + c] * 3.0, (8, 128)) for c in range(3)]

    def on_firsts(firsts, tiles, rows_of_parts):
        mj = [triple(t) for t in tiles]
        for a, ns in firsts:
            g1[a] += lax.dot_general(
                rows_of_parts, beside(ns), (((1,), (1,)), ((), ())), preferred_element_type=f32)
        for a, ns in firsts:
            for g in range(16):
                rows = slice(8 * g, 8 * g + 8)
                sums = [f1[a, c, rows, :] for c in range(3)]
                for q, n in enumerate(ns):
                    h = [hxyz[n, c, rows, :] for c in range(3)]
                    d = dot_rows(h, mj[q])
                    sums = [sums[c] + h[c] * d for c in range(3)]
                for c in range(3):
                    f1[a, c, rows, :] = sums[c]

    def face_list(f):
        return [(face_first(f, p), [FACE + (f * 4 + p) * 4 + q for q in range(4)]) for p in range(4)]

    def edge_list(k):
        return [(edge_first(k, p), [EDGE + (k * 2 + p) * 2 + q for q in range(2)]) for p in range(2)]

    def corner_list(k):
        return [(corner_first(k), [CORNER + k])]

    kinds = ((0, 3, 4, 0, face_list, 1), (3, 9, 2, 12, edge_list, 2), (9, 13, 1, 24, corner_list, 4))

    def send_back(r):
        for low, high, count, start, entries, group in kinds:
            def one(step, carry):
                for k in [step * group + u for u in range(group)]:
                    fields = on_seconds(entries(k))
                    for q in range(count):
                        back[r, start + k * count + q] = tile_field(*fields[q])
                return carry

            lax.fori_loop(0, (high - low) // group, one, 0)
            for m in range(low, high):
                fold_copy(r, m).start()

    def take_halo(r, kind):
        low, high, count, start, entries, group = kinds[kind]

        def one(step, carry):
            for k in [step * group + u for u in range(group)]:
                slots = [start + k * count + q for q in range(count)]
                parts = [mjp[s] for s in slots]
                wide = jnp.concatenate(parts, axis=1) if count > 1 else parts[0]
                on_firsts(entries(k), [halo[r, s] for s in slots], wide)
            return carry

        lax.fori_loop(0, (high - low) // group, one, 0)

    def own_tiles(r):
        f2own[...] = jnp.zeros_like(f2own)
        g2own[...] = jnp.zeros_like(g2own)

        def near(a, carry):
            ns = [OWN + a * 4 + d for d in range(4)]
            bs = [lax.rem(a + d, 8) for d in range(4)]
            tiles = [own[r, b] for b in bs]
            mj = [triple(t) for t in tiles]
            two = jnp.dot(ms[a], beside(ns), preferred_element_type=f32)
            wide = jnp.concatenate([ms[b, :, 0:128] for b in bs[1:]], axis=1)
            g1[a] = lax.dot_general(
                wide, beside(ns[1:]), (((1,), (1,)), ((), ())), preferred_element_type=f32)
            sums = [[jnp.zeros((8, 128), f32)] * 3 for _ in range(4)]
            for g in range(16):
                rows = slice(8 * g, 8 * g + 8)
                m = [mi[a, rows, c * 128 : c * 128 + 128] for c in range(3)]
                first = None
                for d in range(4):
                    h = [hxyz[ns[d], c, rows, :] for c in range(3)]
                    t = dot_rows(h, m)
                    sums[d] = [sums[d][c] + h[c] * t for c in range(3)]
                    if d > 0:
                        t = dot_rows(h, mj[d])
                        add = [h[c] * t for c in range(3)]
                        first = add if first is None else [first[c] + add[c] for c in range(3)]
                for c in range(3):
                    f1[a, c, rows, :] = first[c]
            vec[r, a] = tile_field(sums[0], two[:, 0:128])
            for d in range(1, 4):
                for c in range(3):
                    f2own[bs[d], c] += sums[d][c]
                g2own[bs[d]] += two[:, d * 128 : d * 128 + 128]
            return carry

        lax.fori_loop(0, TILES, near, 0)

        for a in range(4):
            entry = [(a, [LAST + a])]
            fields, parts = on_seconds(entry)[0]
            for c in range(3):
                f2own[a + 4, c] += fields[c]
            g2own[a + 4] += parts
            on_firsts(entry, [own[r, a + 4]], ms[a + 4, :, 0:128])

    def own_sums(r):
        total = jnp.zeros((8, 128), f32)
        for a in range(TILES):
            off = tile_field([f2own[a, c] for c in range(3)], g2own[a])
            total = total + own[r, a] * (vec[r, a] + 2.0 * off)
            vec[r, a] += off
        return total

    def wait_halo(r):
        for m in range(N_MSG):
            halo_copy(r, m).wait_recv()
        for slot in range(N_SLOTS):
            mjp[slot] = two_parts(halo[r, slot])

    def first_sums(r):
        for a in range(TILES):
            sums = [jnp.sum(jnp.transpose(f1[a, c]), axis=0, keepdims=True) for c in range(3)]
            parts = fold_parts(g1[a])
            vec[r, a] += put(*sums) - jnp.where(vec_rows, parts[:, :128] + parts[:, 128:], 0.0)

    def add_folded(r):
        for m in range(N_MSG):
            fold_copy(r, m).wait_recv()
        for slot in range(N_SLOTS):
            vec[r, SLOT_TILE[slot]] += fold[r, slot]

    def phase_copy(phase, k):
        return pltpu.make_async_remote_copy(
            src_ref=ar_send.at[phase], dst_ref=ar_recv.at[phase, k - 1],
            send_sem=as_sem.at[phase, k - 1], recv_sem=ar_sem.at[phase, k - 1],
            device_id=partner(phase, k), device_id_type=MESH)

    def start_phase(phase, total):
        ar_send[phase] = total
        for k in range(1, 8):
            phase_copy(phase, k).start()

    def end_phase(phase):
        total = ar_send[phase]
        for k in range(1, 8):
            phase_copy(phase, k).wait_recv()
            total = total + ar_recv[phase, k - 1]
        return total

    def rows_dot(left, right):
        total = left[0] * right[0]
        for a in range(1, TILES):
            total = total + left[a] * right[a]
        return total

    columns(0)

    def own_near(a, carry):
        for d in range(4):
            coefficients(OWN + a * 4 + d, a, own[0, lax.rem(a + d, 8)], True)
        return carry

    lax.fori_loop(0, 8, own_near, 0)
    for a in range(4):
        coefficients(LAST + a, a, own[0, a + 4], True)
    own_tiles(0)
    own_sums(0)
    wait_halo(0)
    for e, start, count in MESSAGES:
        shift = jnp.where(row == 0, e[0] * BOX_EDGE, 0.0) + jnp.where(
            row == 1, e[1] * BOX_EDGE, 0.0) + jnp.where(row == 2, e[2] * BOX_EDGE, 0.0)
        for slot in range(start, start + count):
            xj[slot] = halo[0, slot] + shift

    def face_one(n, carry):
        f = n // 4
        for q in range(4):
            coefficients(FACE + n * 4 + q, face_first(f, n % 4), xj[f * 4 + q], False)
        return carry

    def edge_one(k, carry):
        for p in range(2):
            for q in range(2):
                coefficients(EDGE + k * 4 + p * 2 + q, edge_first(k, p), xj[12 + k * 2 + q], False)
        return carry

    lax.fori_loop(0, 12, face_one, 0)
    lax.fori_loop(0, 6, edge_one, 0)
    for k in range(4):
        coefficients(CORNER + k, corner_first(k), xj[24 + k], False)
    send_back(0)
    for kind in range(3):
        take_halo(0, kind)
    first_sums(0)
    add_folded(0)

    for r in (1, 2):
        for a in range(TILES):
            own[r, a] = polar8[a] * vec[r - 1, a]
        send_halo(r)
        columns(r)
        send_back(r)
        own_tiles(r)
        g12 = own_sums(r)
        wait_halo(r)
        if r == 2:
            for slot in range(N_SLOTS):
                g12 = g12 + 2.0 * (halo[2, slot] * back[2, slot])
            parts = [
                rows_dot(vec[0], own[1]), rows_dot(vec[1], own[1]), rows_dot(vec[1], own[2]), g12]
            parts = [jnp.sum(g, axis=0, keepdims=True) for g in parts]
            start_phase(0, jnp.where(row == 0, parts[0], jnp.where(
                row == 1, parts[1], jnp.where(row == 2, parts[2], parts[3]))))
        take_halo(r, 0)
        if r == 2:
            start_phase(1, end_phase(0))
        take_halo(r, 1)
        take_halo(r, 2)
        if r == 2:
            start_phase(2, end_phase(1))
        first_sums(r)
        add_folded(r)

    sums = jnp.sum(end_phase(2), axis=1, keepdims=True)
    s00, s01, s11, s12 = (sums[i : i + 1] for i in range(4))
    alpha = s00 / (s00 - s01)
    keep = 1.0 - alpha
    rho = keep * keep * s00 + 2.0 * keep * alpha * s01 + alpha * alpha * s11
    a0 = keep + rho / s00
    a1 = alpha
    denom = (a0 * a0 * s00 + 2.0 * a0 * a1 * s01 + a1 * a1 * s11) - (
        a0 * a0 * s01 + 2.0 * a0 * a1 * s11 + a1 * a1 * s12)
    step = rho / denom
    d0 = 1.0 / SCALE
    d1, d2 = (alpha + step * a0) * d0, step * a1 * d0
    r0, r1, r2 = keep - step * a0, alpha - step * a1 + step * a0, step * a1
    for a in range(TILES):
        dip = d0 * own[0, a] + d1 * own[1, a] + d2 * own[2, a]
        res = r0 * vec[0, a] + r1 * vec[1, a] + r2 * vec[2, a]
        for c in range(3):
            dip_out[8 * c + a : 8 * c + a + 1] = dip[4 + c : 5 + c]
            res_out[8 * c + a : 8 * c + a + 1] = res[4 + c : 5 + c]

    for r in range(3):
        for m in range(N_MSG):
            halo_copy(r, m).wait_send()
            fold_copy(r, m).wait_send()
    for phase in range(3):
        for k in range(1, 8):
            phase_copy(phase, k).wait_send()


def solution(mesh):
    sizes = tuple(mesh.shape[a] for a in AXES)
    f32, bf16 = jnp.float32, jnp.bfloat16

    def shards(positions, polar, field, groups, pair_tiles):
        vmem = pl.BlockSpec(memory_space=pltpu.VMEM)
        dma = pltpu.SemaphoreType.DMA
        scratch = [
            pltpu.VMEM((ENTRIES, 3, 128, 128), f32),
            pltpu.VMEM((ENTRIES, 256, 128), bf16),
            pltpu.VMEM((8, 128, 640), f32),
            pltpu.VMEM((8, 128, 384), f32),
            pltpu.VMEM((8, 16, 256), bf16),
            pltpu.VMEM((N_SLOTS, 16, 128), bf16),
            pltpu.VMEM((8, 3, 128, 128), f32),
            pltpu.VMEM((8, 16, 256), f32),
            pltpu.VMEM((8, 3, 8, 128), f32),
            pltpu.VMEM((8, 16, 128), f32),
            pltpu.VMEM((ENTRIES, 128), f32),
            pltpu.VMEM((N_SLOTS, 8, 128), f32),
            pltpu.VMEM((3, 8, 8, 128), f32),
            pltpu.VMEM((3, 8, 8, 128), f32),
            pltpu.VMEM((8, 8, 128), f32),
            pltpu.VMEM((3, N_SLOTS, 8, 128), f32),
            pltpu.VMEM((3, N_SLOTS, 8, 128), f32),
            pltpu.VMEM((3, N_SLOTS, 8, 128), f32),
            pltpu.VMEM((3, N_SLOTS, 8, 128), f32),
            pltpu.VMEM((3, 8, 128), f32),
            pltpu.VMEM((3, 7, 8, 128), f32),
            dma((3, N_MSG)), dma((3, N_MSG)), dma((3, N_MSG)), dma((3, N_MSG)),
            dma((3, 7)), dma((3, 7)),
        ]
        atoms = positions.shape[-1]
        rows = atoms // TILE
        out = jax.ShapeDtypeStruct((3 * rows, TILE), f32)
        dip, res = pl.pallas_call(
            functools.partial(kernel, sizes),
            out_shape=(out, out),
            in_specs=[vmem] * 6,
            out_specs=(vmem, vmem),
            scratch_shapes=scratch,
            compiler_params=pltpu.CompilerParams(
                collective_id=0, has_side_effects=True, vmem_limit_bytes=50 * 1024 * 1024),
            name="dipole_cg",
        )(positions.reshape(3 * rows, TILE), polar.reshape(rows, TILE), field.reshape(3 * rows, TILE),
          groups.reshape(rows, TILE), pair_tiles.reshape(3, 1, -1), jnp.asarray(KEYS))
        return dip.reshape(1, 1, 1, 3, atoms), res.reshape(1, 1, 1, 3, atoms)

    placed = (
        P(*AXES, None, None), P(*AXES, None), P(*AXES, None, None), P(*AXES, None), P(*AXES, None, None))
    return jax.shard_map(
        shards, mesh=mesh, in_specs=placed, out_specs=(placed[0], placed[0]), check_vma=False)
```

```python
import functools

import jax
import jax.numpy as jnp
import numpy as np
from jax import lax
from jax.experimental import pallas as pl
from jax.experimental.pallas import tpu as pltpu
from jax.sharding import PartitionSpec as P

TILE = 128
TILES = 8
AXES = ("gx", "gy", "gz")
BOX_EDGE = 21.7
THOLE_A = 0.39
FAR = 1000.0
SCALE = 3.0 / 16.0
C10 = np.float32(10.0 / 3.0)
C8 = np.float32(5.0) - (C10 - np.float32(1.0))
MESH = pl.DeviceIdType.MESH
SHELL = [
    (0, 0, 0), (0, 0, 1), (0, 1, -1), (0, 1, 0), (0, 1, 1), (1, -1, -1), (1, -1, 0),
    (1, -1, 1), (1, 0, -1), (1, 0, 0), (1, 0, 1), (1, 1, -1), (1, 1, 0), (1, 1, 1),
]
N_SLOTS = 28
FACE, EDGE, CORNER, OWN, LAST = 0, 48, 72, 76, 108
ENTRIES = 112


def face_first(f, p):
    s = 1 + f + f * (f - 1) // 2
    return p // s * (2 * s) + s + p % s


def edge_first(k, p):
    g, sg = k // 2, k % 2
    free = 4 - 2 * g + g * (g - 1) // 2
    return free * p + 4 - 2 * ((2 - g) // 2) + (1 + g // 2) * sg


def corner_first(k):
    return 4 + k


def tables():
    messages, slot_tile, keys = [], [], []
    for f in range(3):
        s = 1 << f
        e = [0, 0, 0]
        e[2 - f] = 1
        messages.append((tuple(e), len(slot_tile), 4))
        slot_tile += [q // s * 2 * s + q % s for q in range(4)]
    for k in range(6):
        g, sg = k // 2, k % 2
        e = [[0, 1, 2 * sg - 1], [1, 0, 2 * sg - 1], [1, 2 * sg - 1, 0]][g]
        free, low = (4, 2, 1)[g], (1, 1, 2)[g]
        messages.append((tuple(e), len(slot_tile), 2))
        slot_tile += [free * q + low * (1 - sg) for q in range(2)]
    for k in range(4):
        sy, sz = k // 2, k % 2
        messages.append(((1, 2 * sy - 1, 2 * sz - 1), len(slot_tile), 1))
        slot_tile += [2 * (1 - sy) + 1 - sz]
    for m, (e, start, count) in enumerate(messages):
        for p in range(count):
            if m < 3:
                a = face_first(m, p)
            elif m < 9:
                a = edge_first(m - 3, p)
            else:
                a = corner_first(m - 9)
            keys += [(a, SHELL.index(e), slot_tile[start + q]) for q in range(count)]
    for a in range(8):
        for d in range(4):
            b = (a + d) % 8
            keys.append((min(a, b), 0, max(a, b)))
    keys += [(a, 0, a + 4) for a in range(4)]
    assert len(set(keys)) == ENTRIES
    key = np.array([a * 128 + c * 8 + b for a, c, b in keys], np.int32)
    return messages, slot_tile, np.ascontiguousarray(np.broadcast_to(key[:, None], (ENTRIES, 128)))


MESSAGES, SLOT_TILE, KEYS = tables()
N_MSG = len(MESSAGES)


def halves(tile):
    hi = tile.astype(jnp.bfloat16).astype(jnp.float32)
    return hi, (tile - hi)


def two_parts(tile):
    hi, rest = halves(tile)
    return jnp.concatenate([hi, rest], axis=0).astype(jnp.bfloat16)


def fold_parts(parts):
    return parts[0:8] + parts[8:16]


def kernel(sizes, pos_in, pol_in, fld_in, grp_in, prs_in, keys_in, dip_out, res_out,
           pos, pol, fld, grp, prs, keys, hxyz, c3p, xi, mi, ms, mjp, f1, g1, f2own, g2own, flag, xj,
           own, vec, polar8, send, halo, back, fold, ar_send, ar_recv,
           in_sem, hs_sem, hr_sem, fs_sem, fr_sem, as_sem, ar_sem):
    f32, bf16 = jnp.float32, jnp.bfloat16
    me = tuple(lax.axis_index(a) for a in AXES)
    gx, gy, gz = me

    def at(e):
        return tuple(lax.rem(m + d + n, n) for m, d, n in zip(me, e, sizes))

    core, zed = lax.rem(gy, 2), gy // 2

    def partner(phase, k):
        if phase == 0:
            j = lax.rem(core * 4 + gz + k, 8)
            return (gx, gy - core + j // 4, lax.rem(j, 4))
        if phase == 1:
            return (lax.rem(gx + k, 8), gy, gz)
        return (gx, lax.rem(zed + k, 8) * 2 + core, gz)

    arguments = (pos_in, pol_in, fld_in, grp_in, prs_in, keys_in)
    taken = [
        pltpu.make_async_copy(src, dst, in_sem.at[i])
        for i, (src, dst) in enumerate(zip(arguments, (pos, pol, fld, grp, prs, keys)))]
    for copy in taken:
        copy.start()

    barrier = pltpu.get_barrier_semaphore()
    signals = 0
    for e, _, _ in MESSAGES:
        for sign in (1, -1):
            pl.semaphore_signal(barrier, inc=1, device_id=at(tuple(sign * d for d in e)), device_id_type=MESH)
            signals += 1
    for phase in range(3):
        for k in range(1, 8):
            pl.semaphore_signal(barrier, inc=1, device_id=partner(phase, k), device_id_type=MESH)
            signals += 1

    row = lax.broadcasted_iota(jnp.int32, (8, 128), 0)
    vec_rows = jnp.logical_and(row >= 4, row < 7)

    def put(x, y, z):
        return jnp.where(row == 4, x, jnp.where(row == 5, y, jnp.where(row == 6, z, 0.0)))

    def tile_field(sums, parts):
        rows = [jnp.sum(f, axis=0, keepdims=True) for f in sums]
        return put(*rows) - jnp.where(vec_rows, fold_parts(parts), 0.0)

    for copy in taken:
        copy.wait()

    for a in range(TILES):
        p = pol[a : a + 1]
        polar8[a] = jnp.broadcast_to(p * SCALE, (8, 128))
        own[0, a] = jnp.concatenate(
            [pos[8 * c + a : 8 * c + a + 1] for c in range(3)] + [lax.rsqrt(p)]
            + [p * SCALE * fld[8 * c + a : 8 * c + a + 1] for c in range(3)]
            + [grp[a : a + 1].astype(f32)], axis=0)

    def halo_copy(r, m):
        e, start, count = MESSAGES[m]
        return pltpu.make_async_remote_copy(
            src_ref=send.at[r, pl.ds(start, count)], dst_ref=halo.at[r, pl.ds(start, count)],
            send_sem=hs_sem.at[r, m], recv_sem=hr_sem.at[r, m],
            device_id=at(tuple(-d for d in e)), device_id_type=MESH)

    def fold_copy(r, m):
        e, start, count = MESSAGES[m]
        return pltpu.make_async_remote_copy(
            src_ref=back.at[r, pl.ds(start, count)], dst_ref=fold.at[r, pl.ds(start, count)],
            send_sem=fs_sem.at[r, m], recv_sem=fr_sem.at[r, m],
            device_id=at(e), device_id_type=MESH)

    def send_halo(r):
        for slot in range(N_SLOTS):
            send[r, slot] = own[r, SLOT_TILE[slot]]
        if r == 0:
            pl.semaphore_wait(barrier, signals)
        for m in reversed(range(N_MSG)):
            halo_copy(r, m).start()

    send_halo(0)

    key_row = prs[0] * 128 + prs[1] * 8 + prs[2]
    hit = jnp.where(keys[:, : key_row.shape[1]] == key_row, 0.0, FAR)
    flag[...] = jnp.broadcast_to(jnp.min(hit, axis=1, keepdims=True), (ENTRIES, 128))

    def columns(r):
        cols = jnp.transpose(own[r].reshape(64, 128))
        for a in range(TILES):
            def wide(k, scale):
                return jnp.broadcast_to(cols[:, a * 8 + k : a * 8 + k + 1] * scale, (128, 128))

            for c in range(3):
                mi[a, :, c * 128 : c * 128 + 128] = wide(4 + c, 3.0)
            if r == 0:
                for c in range(3):
                    xi[a, :, c * 128 : c * 128 + 128] = wide(c, 1.0)
                xi[a, :, 384:512] = wide(3, -THOLE_A)
                xi[a, :, 512:640] = wide(7, 1.0)
            parts = two_parts(own[r, a])
            ms[a] = jnp.concatenate([parts, parts], axis=1)

    def coefficients(n, a, tile, grouped):
        shift = flag[pl.ds(n, 1), :]
        xs = [jnp.broadcast_to(tile[c : c + 1], (16, 128)) for c in range(4)]
        xs[0] = xs[0] + jnp.broadcast_to(shift, (16, 128))
        group = jnp.broadcast_to(tile[7:8], (16, 128))
        for g in range(8):
            rows = slice(16 * g, 16 * g + 16)
            s = [xs[c] - xi[a, rows, c * 128 : c * 128 + 128] for c in range(3)]
            r2 = s[0] * s[0] + s[1] * s[1] + s[2] * s[2]
            if grouped:
                r2 = jnp.where(xi[a, rows, 512:640] == group, FAR * FAR, r2)
            rinv = lax.rsqrt(r2)
            r = r2 * rinv
            x = r2 * r * (xi[a, rows, 384:512] * xs[3])
            ex = jnp.exp(x)
            l3 = 1.0 - ex
            v = jnp.clip(r - 8.0, -1.0, 1.0)
            v2 = v * v
            cut = jnp.maximum(C8 - v * ((v2 - C10) * v2 + 5.0), 0.0)
            w = cut * (rinv * rinv * rinv)
            c3 = w * l3
            q2 = w * (l3 + x * ex)
            q = q2 * lax.rsqrt(jnp.maximum(q2, 1e-36)) * rinv
            for c in range(3):
                hxyz[n, c, rows, :] = q * s[c]
            hi = c3.astype(bf16)
            c3p[n, rows, :] = hi
            c3p[n, 128 + 16 * g : 144 + 16 * g, :] = (c3 - hi.astype(f32)).astype(bf16)

    def beside(ns):
        return jnp.concatenate([c3p[n] for n in ns], axis=1) if len(ns) > 1 else c3p[ns[0]]

    def dot_rows(h, m):
        return h[0] * m[0] + h[1] * m[1] + h[2] * m[2]

    def on_seconds(firsts):
        count = len(firsts[0][1])
        sums, parts = [None] * count, None
        for a, ns in firsts:
            part = jnp.dot(ms[a], beside(ns), preferred_element_type=f32)
            parts = part if parts is None else parts + part
        for a, ns in firsts:
            for g in range(16):
                rows = slice(8 * g, 8 * g + 8)
                m = [mi[a, rows, c * 128 : c * 128 + 128] for c in range(3)]
                for q in range(count):
                    h = [hxyz[ns[q], c, rows, :] for c in range(3)]
                    d = dot_rows(h, m)
                    add = [h[c] * d for c in range(3)]
                    sums[q] = add if sums[q] is None else [sums[q][c] + add[c] for c in range(3)]
        return [(sums[q], parts[:, q * 128 : q * 128 + 128]) for q in range(count)]

    def triple(tile):
        return [jnp.broadcast_to(tile[4 + c : 5 + c] * 3.0, (8, 128)) for c in range(3)]

    def on_firsts(firsts, tiles, rows_of_parts):
        mj = [triple(t) for t in tiles]
        for a, ns in firsts:
            g1[a] += lax.dot_general(
                rows_of_parts, beside(ns), (((1,), (1,)), ((), ())), preferred_element_type=f32)
        for a, ns in firsts:
            for g in range(16):
                rows = slice(8 * g, 8 * g + 8)
                sums = [f1[a, c, rows, :] for c in range(3)]
                for q, n in enumerate(ns):
                    h = [hxyz[n, c, rows, :] for c in range(3)]
                    d = dot_rows(h, mj[q])
                    sums = [sums[c] + h[c] * d for c in range(3)]
                for c in range(3):
                    f1[a, c, rows, :] = sums[c]

    def face_list(f):
        return [(face_first(f, p), [FACE + (f * 4 + p) * 4 + q for q in range(4)]) for p in range(4)]

    def edge_list(k):
        return [(edge_first(k, p), [EDGE + (k * 2 + p) * 2 + q for q in range(2)]) for p in range(2)]

    def corner_list(k):
        return [(corner_first(k), [CORNER + k])]

    kinds = ((0, 3, 4, 0, face_list, 1), (3, 9, 2, 12, edge_list, 2), (9, 13, 1, 24, corner_list, 4))

    def send_back(r, kind):
        low, high, count, start, entries, group = kinds[kind]

        def one(step, carry):
            for k in [step * group + u for u in range(group)]:
                fields = on_seconds(entries(k))
                for q in range(count):
                    back[r, start + k * count + q] = tile_field(*fields[q])
            return carry

        lax.fori_loop(0, (high - low) // group, one, 0)
        for m in range(low, high):
            fold_copy(r, m).start()

    def take_halo(r, kind):
        low, high, count, start, entries, group = kinds[kind]

        def one(step, carry):
            for k in [step * group + u for u in range(group)]:
                slots = [start + k * count + q for q in range(count)]
                parts = [mjp[s] for s in slots]
                wide = jnp.concatenate(parts, axis=1) if count > 1 else parts[0]
                on_firsts(entries(k), [halo[r, s] for s in slots], wide)
            return carry

        lax.fori_loop(0, (high - low) // group, one, 0)

    def own_tiles(r, seconds, firsts):
        def near(a, carry):
            ns = [OWN + a * 4 + d for d in range(4)]
            bs = [lax.rem(a + d, 8) for d in range(4)]
            if seconds:
                two = jnp.dot(ms[a], beside(ns), preferred_element_type=f32)
            if firsts:
                mj = [triple(own[r, b]) for b in bs]
                wide = jnp.concatenate([ms[b, :, 0:128] for b in bs[1:]], axis=1)
                g1[a] = lax.dot_general(
                    wide, beside(ns[1:]), (((1,), (1,)), ((), ())), preferred_element_type=f32)
            sums = [[jnp.zeros((8, 128), f32)] * 3 for _ in range(4)]
            for g in range(16):
                rows = slice(8 * g, 8 * g + 8)
                m = [mi[a, rows, c * 128 : c * 128 + 128] for c in range(3)]
                first = None
                for d in range(4):
                    if d == 0 and not seconds:
                        continue
                    h = [hxyz[ns[d], c, rows, :] for c in range(3)]
                    if seconds:
                        t = dot_rows(h, m)
                        sums[d] = [sums[d][c] + h[c] * t for c in range(3)]
                    if firsts and d > 0:
                        t = dot_rows(h, mj[d])
                        add = [h[c] * t for c in range(3)]
                        first = add if first is None else [first[c] + add[c] for c in range(3)]
                if firsts:
                    for c in range(3):
                        f1[a, c, rows, :] = first[c]
            if seconds:
                vec[r, a] = tile_field(sums[0], two[:, 0:128])
                for d in range(1, 4):
                    for c in range(3):
                        f2own[bs[d], c] += sums[d][c]
                    g2own[bs[d]] += two[:, d * 128 : d * 128 + 128]
            return carry

        if seconds:
            f2own[...] = jnp.zeros_like(f2own)
            g2own[...] = jnp.zeros_like(g2own)
        lax.fori_loop(0, TILES, near, 0)
        for a in range(4):
            entry = [(a, [LAST + a])]
            if seconds:
                fields, parts = on_seconds(entry)[0]
                for c in range(3):
                    f2own[a + 4, c] += fields[c]
                g2own[a + 4] += parts
            if firsts:
                on_firsts(entry, [own[r, a + 4]], ms[a + 4, :, 0:128])

    def own_sums(r):
        total = jnp.zeros((8, 128), f32)
        for a in range(TILES):
            off = tile_field([f2own[a, c] for c in range(3)], g2own[a])
            total = total + own[r, a] * (vec[r, a] + 2.0 * off)
            vec[r, a] += off
        return total

    def wait_halo(r):
        for m in range(N_MSG):
            halo_copy(r, m).wait_recv()
        for slot in range(N_SLOTS):
            mjp[slot] = two_parts(halo[r, slot])

    def first_sums(r):
        for a in range(TILES):
            sums = [jnp.sum(jnp.transpose(f1[a, c]), axis=0, keepdims=True) for c in range(3)]
            parts = fold_parts(g1[a])
            vec[r, a] += put(*sums) - jnp.where(vec_rows, parts[:, :128] + parts[:, 128:], 0.0)

    def add_folded(r):
        for m in range(N_MSG):
            fold_copy(r, m).wait_recv()
        for slot in range(N_SLOTS):
            vec[r, SLOT_TILE[slot]] += fold[r, slot]

    def phase_copy(phase, k):
        return pltpu.make_async_remote_copy(
            src_ref=ar_send.at[phase], dst_ref=ar_recv.at[phase, k - 1],
            send_sem=as_sem.at[phase, k - 1], recv_sem=ar_sem.at[phase, k - 1],
            device_id=partner(phase, k), device_id_type=MESH)

    def start_phase(phase, total):
        ar_send[phase] = total
        for k in range(1, 8):
            phase_copy(phase, k).start()

    def end_phase(phase):
        total = ar_send[phase]
        for k in range(1, 8):
            phase_copy(phase, k).wait_recv()
            total = total + ar_recv[phase, k - 1]
        return total

    def rows_dot(left, right):
        total = left[0] * right[0]
        for a in range(1, TILES):
            total = total + left[a] * right[a]
        return total

    columns(0)

    def own_near(a, carry):
        for d in range(4):
            coefficients(OWN + a * 4 + d, a, own[0, lax.rem(a + d, 8)], True)
        return carry

    lax.fori_loop(0, 8, own_near, 0)
    for a in range(4):
        coefficients(LAST + a, a, own[0, a + 4], True)
    wait_halo(0)
    for e, start, count in MESSAGES:
        shift = jnp.where(row == 0, e[0] * BOX_EDGE, 0.0) + jnp.where(
            row == 1, e[1] * BOX_EDGE, 0.0) + jnp.where(row == 2, e[2] * BOX_EDGE, 0.0)
        for slot in range(start, start + count):
            xj[slot] = halo[0, slot] + shift

    def face_one(n, carry):
        f = n // 4
        for q in range(4):
            coefficients(FACE + n * 4 + q, face_first(f, n % 4), xj[f * 4 + q], False)
        return carry

    def edge_one(k, carry):
        for p in range(2):
            for q in range(2):
                coefficients(EDGE + k * 4 + p * 2 + q, edge_first(k, p), xj[12 + k * 2 + q], False)
        return carry

    for k in range(4):
        coefficients(CORNER + k, corner_first(k), xj[24 + k], False)
    send_back(0, 2)
    lax.fori_loop(0, 6, edge_one, 0)
    send_back(0, 1)
    lax.fori_loop(0, 12, face_one, 0)
    send_back(0, 0)
    own_tiles(0, True, True)
    own_sums(0)
    for kind in range(3):
        take_halo(0, kind)
    first_sums(0)
    add_folded(0)

    for r in (1, 2):
        for a in range(TILES):
            own[r, a] = polar8[a] * vec[r - 1, a]
        send_halo(r)
        columns(r)
        for kind in (2, 1, 0):
            send_back(r, kind)
        own_tiles(r, True, r == 1)
        g12 = own_sums(r)
        wait_halo(r)
        if r == 2:
            for slot in range(N_SLOTS):
                g12 = g12 + 2.0 * (halo[2, slot] * back[2, slot])
            parts = [
                rows_dot(vec[0], own[1]), rows_dot(vec[1], own[1]), rows_dot(vec[1], own[2]), g12]
            parts = [jnp.sum(jnp.sum(g, axis=0, keepdims=True), axis=1, keepdims=True) for g in parts]
            lane = lax.broadcasted_iota(jnp.int32, (1, 128), 1)
            start_phase(0, jnp.where(lane == 0, parts[0], jnp.where(
                lane == 1, parts[1], jnp.where(lane == 2, parts[2], parts[3]))))
            own_tiles(2, False, True)
        take_halo(r, 0)
        if r == 2:
            start_phase(1, end_phase(0))
        take_halo(r, 1)
        take_halo(r, 2)
        first_sums(r)
        if r == 2:
            start_phase(2, end_phase(1))
        add_folded(r)

    sums = end_phase(2)
    s00, s01, s11, s12 = (sums[:, i : i + 1] for i in range(4))
    alpha = s00 / (s00 - s01)
    keep = 1.0 - alpha
    rho = keep * keep * s00 + 2.0 * keep * alpha * s01 + alpha * alpha * s11
    a0 = keep + rho / s00
    a1 = alpha
    denom = (a0 * a0 * s00 + 2.0 * a0 * a1 * s01 + a1 * a1 * s11) - (
        a0 * a0 * s01 + 2.0 * a0 * a1 * s11 + a1 * a1 * s12)
    step = rho / denom
    d0 = 1.0 / SCALE
    d1, d2 = (alpha + step * a0) * d0, step * a1 * d0
    r0, r1, r2 = keep - step * a0, alpha - step * a1 + step * a0, step * a1
    for a in range(TILES):
        dip = d0 * own[0, a] + d1 * own[1, a] + d2 * own[2, a]
        res = r0 * vec[0, a] + r1 * vec[1, a] + r2 * vec[2, a]
        for c in range(3):
            dip_out[8 * c + a : 8 * c + a + 1] = dip[4 + c : 5 + c]
            res_out[8 * c + a : 8 * c + a + 1] = res[4 + c : 5 + c]

    for r in range(3):
        for m in range(N_MSG):
            halo_copy(r, m).wait_send()
            fold_copy(r, m).wait_send()
    for phase in range(3):
        for k in range(1, 8):
            phase_copy(phase, k).wait_send()


def solution(mesh):
    sizes = tuple(mesh.shape[a] for a in AXES)
    f32, bf16 = jnp.float32, jnp.bfloat16

    def shards(positions, polar, field, groups, pair_tiles):
        vmem = pl.BlockSpec(memory_space=pltpu.VMEM)
        anywhere = pl.BlockSpec(memory_space=pl.ANY)
        dma = pltpu.SemaphoreType.DMA
        atoms = positions.shape[-1]
        rows = atoms // TILE
        scratch = [
            pltpu.VMEM((3 * rows, TILE), f32),
            pltpu.VMEM((rows, TILE), f32),
            pltpu.VMEM((3 * rows, TILE), f32),
            pltpu.VMEM((rows, TILE), jnp.int32),
            pltpu.VMEM((3, 1, pair_tiles.shape[-1]), jnp.int32),
            pltpu.VMEM((ENTRIES, 128), jnp.int32),
            pltpu.VMEM((ENTRIES, 3, 128, 128), f32),
            pltpu.VMEM((ENTRIES, 256, 128), bf16),
            pltpu.VMEM((8, 128, 640), f32),
            pltpu.VMEM((8, 128, 384), f32),
            pltpu.VMEM((8, 16, 256), bf16),
            pltpu.VMEM((N_SLOTS, 16, 128), bf16),
            pltpu.VMEM((8, 3, 128, 128), f32),
            pltpu.VMEM((8, 16, 256), f32),
            pltpu.VMEM((8, 3, 8, 128), f32),
            pltpu.VMEM((8, 16, 128), f32),
            pltpu.VMEM((ENTRIES, 128), f32),
            pltpu.VMEM((N_SLOTS, 8, 128), f32),
            pltpu.VMEM((3, 8, 8, 128), f32),
            pltpu.VMEM((3, 8, 8, 128), f32),
            pltpu.VMEM((8, 8, 128), f32),
            pltpu.VMEM((3, N_SLOTS, 8, 128), f32),
            pltpu.VMEM((3, N_SLOTS, 8, 128), f32),
            pltpu.VMEM((3, N_SLOTS, 8, 128), f32),
            pltpu.VMEM((3, N_SLOTS, 8, 128), f32),
            pltpu.VMEM((3, 1, 128), f32),
            pltpu.VMEM((3, 7, 1, 128), f32),
            dma((6,)),
            dma((3, N_MSG)), dma((3, N_MSG)), dma((3, N_MSG)), dma((3, N_MSG)),
            dma((3, 7)), dma((3, 7)),
        ]
        out = jax.ShapeDtypeStruct((3 * rows, TILE), f32)
        dip, res = pl.pallas_call(
            functools.partial(kernel, sizes),
            out_shape=(out, out),
            in_specs=[anywhere] * 6,
            out_specs=(vmem, vmem),
            scratch_shapes=scratch,
            compiler_params=pltpu.CompilerParams(
                collective_id=0, has_side_effects=True, vmem_limit_bytes=64 * 1024 * 1024),
            name="dipole_cg",
        )(positions.reshape(3 * rows, TILE), polar.reshape(rows, TILE), field.reshape(3 * rows, TILE),
          groups.reshape(rows, TILE), pair_tiles.reshape(3, 1, -1), jnp.asarray(KEYS))
        return dip.reshape(1, 1, 1, 3, atoms), res.reshape(1, 1, 1, 3, atoms)

    placed = (
        P(*AXES, None, None), P(*AXES, None), P(*AXES, None, None), P(*AXES, None), P(*AXES, None, None))
    return jax.shard_map(
        shards, mesh=mesh, in_specs=placed, out_specs=(placed[0], placed[0]), check_vma=False)
```

```python
import functools

import jax
import jax.numpy as jnp
import numpy as np
from jax import lax
from jax.experimental import pallas as pl
from jax.experimental.pallas import tpu as pltpu
from jax.sharding import PartitionSpec as P

TILE = 128
TILES = 8
AXES = ("gx", "gy", "gz")
BOX_EDGE = 21.7
THOLE_A = 0.39
FAR = 1000.0
SCALE = 3.0 / 16.0
C10 = np.float32(10.0 / 3.0)
C8 = np.float32(5.0) - (C10 - np.float32(1.0))
MESH = pl.DeviceIdType.MESH
SHELL = [
    (0, 0, 0), (0, 0, 1), (0, 1, -1), (0, 1, 0), (0, 1, 1), (1, -1, -1), (1, -1, 0),
    (1, -1, 1), (1, 0, -1), (1, 0, 0), (1, 0, 1), (1, 1, -1), (1, 1, 0), (1, 1, 1),
]
N_SLOTS = 28
FACE, EDGE, CORNER, OWN, LAST = 0, 48, 72, 76, 108
ENTRIES = 112


def face_first(f, p):
    s = 1 + f + f * (f - 1) // 2
    return p // s * (2 * s) + s + p % s


def edge_first(k, p):
    g, sg = k // 2, k % 2
    free = 4 - 2 * g + g * (g - 1) // 2
    return free * p + 4 - 2 * ((2 - g) // 2) + (1 + g // 2) * sg


def corner_first(k):
    return 4 + k


def tables():
    messages, slot_tile, keys = [], [], []
    for f in range(3):
        s = 1 << f
        e = [0, 0, 0]
        e[2 - f] = 1
        messages.append((tuple(e), len(slot_tile), 4))
        slot_tile += [q // s * 2 * s + q % s for q in range(4)]
    for k in range(6):
        g, sg = k // 2, k % 2
        e = [[0, 1, 2 * sg - 1], [1, 0, 2 * sg - 1], [1, 2 * sg - 1, 0]][g]
        free, low = (4, 2, 1)[g], (1, 1, 2)[g]
        messages.append((tuple(e), len(slot_tile), 2))
        slot_tile += [free * q + low * (1 - sg) for q in range(2)]
    for k in range(4):
        sy, sz = k // 2, k % 2
        messages.append(((1, 2 * sy - 1, 2 * sz - 1), len(slot_tile), 1))
        slot_tile += [2 * (1 - sy) + 1 - sz]
    for m, (e, start, count) in enumerate(messages):
        for p in range(count):
            if m < 3:
                a = face_first(m, p)
            elif m < 9:
                a = edge_first(m - 3, p)
            else:
                a = corner_first(m - 9)
            keys += [(a, SHELL.index(e), slot_tile[start + q]) for q in range(count)]
    for a in range(8):
        for d in range(4):
            b = (a + d) % 8
            keys.append((min(a, b), 0, max(a, b)))
    keys += [(a, 0, a + 4) for a in range(4)]
    assert len(set(keys)) == ENTRIES
    key = np.array([a * 128 + c * 8 + b for a, c, b in keys], np.int32)
    return messages, slot_tile, np.ascontiguousarray(np.broadcast_to(key[:, None], (ENTRIES, 128)))


MESSAGES, SLOT_TILE, KEYS = tables()
N_MSG = len(MESSAGES)


def halves(tile):
    hi = tile.astype(jnp.bfloat16).astype(jnp.float32)
    return hi, (tile - hi)


def two_parts(tile):
    hi, rest = halves(tile)
    return jnp.concatenate([hi, rest], axis=0).astype(jnp.bfloat16)


def fold_parts(parts):
    return parts[0:8] + parts[8:16]


def kernel(sizes, pos_in, pol_in, fld_in, grp_in, prs_in, keys_in, out,
           pos, pol, fld, grp, prs, keys, hxyz, c3p, xi, mi, ms, mjp, f1, g1, f2own, g2own, flag, xj,
           own, vec, polar8, send, halo, back, fold, ar_send, ar_recv,
           in_sem, hs_sem, hr_sem, fs_sem, fr_sem, as_sem, ar_sem):
    f32, bf16 = jnp.float32, jnp.bfloat16
    me = tuple(lax.axis_index(a) for a in AXES)
    gx, gy, gz = me

    def at(e):
        return tuple(lax.rem(m + d + n, n) for m, d, n in zip(me, e, sizes))

    core, zed = lax.rem(gy, 2), gy // 2

    def partner(phase, k):
        if phase == 0:
            j = lax.rem(core * 4 + gz + k, 8)
            return (gx, gy - core + j // 4, lax.rem(j, 4))
        if phase == 1:
            return (lax.rem(gx + k, 8), gy, gz)
        return (gx, lax.rem(zed + k, 8) * 2 + core, gz)

    arguments = (pos_in, pol_in, fld_in, grp_in, prs_in, keys_in)
    taken = [
        pltpu.make_async_copy(src, dst, in_sem.at[i])
        for i, (src, dst) in enumerate(zip(arguments, (pos, pol, fld, grp, prs, keys)))]
    for copy in taken:
        copy.start()

    barrier = pltpu.get_barrier_semaphore()
    signals = 0
    for e, _, _ in MESSAGES:
        for sign in (1, -1):
            pl.semaphore_signal(barrier, inc=1, device_id=at(tuple(sign * d for d in e)), device_id_type=MESH)
            signals += 1
    for phase in range(3):
        for k in range(1, 8):
            pl.semaphore_signal(barrier, inc=1, device_id=partner(phase, k), device_id_type=MESH)
            signals += 1

    row = lax.broadcasted_iota(jnp.int32, (8, 128), 0)
    vec_rows = jnp.logical_and(row >= 4, row < 7)

    def put(x, y, z):
        return jnp.where(row == 4, x, jnp.where(row == 5, y, jnp.where(row == 6, z, 0.0)))

    def tile_field(sums, parts):
        rows = [jnp.sum(f, axis=0, keepdims=True) for f in sums]
        return put(*rows) - jnp.where(vec_rows, fold_parts(parts), 0.0)

    for copy in taken:
        copy.wait()

    for a in range(TILES):
        p = pol[a : a + 1]
        polar8[a] = jnp.broadcast_to(p * SCALE, (8, 128))
        own[0, a] = jnp.concatenate(
            [pos[8 * c + a : 8 * c + a + 1] for c in range(3)] + [lax.rsqrt(p)]
            + [p * SCALE * fld[8 * c + a : 8 * c + a + 1] for c in range(3)]
            + [grp[a : a + 1].astype(f32)], axis=0)

    def halo_copy(r, m):
        e, start, count = MESSAGES[m]
        return pltpu.make_async_remote_copy(
            src_ref=send.at[r, pl.ds(start, count)], dst_ref=halo.at[r, pl.ds(start, count)],
            send_sem=hs_sem.at[r, m], recv_sem=hr_sem.at[r, m],
            device_id=at(tuple(-d for d in e)), device_id_type=MESH)

    def fold_copy(r, m):
        e, start, count = MESSAGES[m]
        return pltpu.make_async_remote_copy(
            src_ref=back.at[r, pl.ds(start, count)], dst_ref=fold.at[r, pl.ds(start, count)],
            send_sem=fs_sem.at[r, m], recv_sem=fr_sem.at[r, m],
            device_id=at(e), device_id_type=MESH)

    def send_halo(r):
        for slot in range(N_SLOTS):
            send[r, slot] = own[r, SLOT_TILE[slot]]
        if r == 0:
            pl.semaphore_wait(barrier, signals)
        for m in reversed(range(N_MSG)):
            halo_copy(r, m).start()

    send_halo(0)

    key_row = prs[0] * 128 + prs[1] * 8 + prs[2]
    hit = jnp.where(keys[:, : key_row.shape[1]] == key_row, 0.0, FAR)
    flag[...] = jnp.broadcast_to(jnp.min(hit, axis=1, keepdims=True), (ENTRIES, 128))

    def columns(r):
        cols = jnp.transpose(own[r].reshape(64, 128))
        for a in range(TILES):
            def wide(k, scale):
                return jnp.broadcast_to(cols[:, a * 8 + k : a * 8 + k + 1] * scale, (128, 128))

            for c in range(3):
                mi[a, :, c * 128 : c * 128 + 128] = wide(4 + c, 3.0)
            if r == 0:
                for c in range(3):
                    xi[a, :, c * 128 : c * 128 + 128] = wide(c, 1.0)
                xi[a, :, 384:512] = wide(3, -THOLE_A)
                xi[a, :, 512:640] = wide(7, 1.0)
            parts = two_parts(own[r, a])
            ms[a] = jnp.concatenate([parts, parts], axis=1)

    def coefficients(n, a, tile, grouped):
        shift = flag[pl.ds(n, 1), :]
        xs = [tile[c : c + 1] for c in range(4)]
        xs[0] = xs[0] + shift
        group = tile[7:8]
        s = [xs[c] - xi[a, :, c * 128 : c * 128 + 128] for c in range(3)]
        r2 = s[0] * s[0] + s[1] * s[1] + s[2] * s[2]
        if grouped:
            r2 = jnp.where(xi[a, :, 512:640] == group, FAR * FAR, r2)
        rinv = lax.rsqrt(r2)
        r = r2 * rinv
        x = r2 * r * (xi[a, :, 384:512] * xs[3])
        ex = jnp.exp(x)
        l3 = 1.0 - ex
        v = jnp.clip(r - 8.0, -1.0, 1.0)
        v2 = v * v
        cut = jnp.maximum(C8 - v * ((v2 - C10) * v2 + 5.0), 0.0)
        w = cut * (rinv * rinv * rinv)
        c3 = w * l3
        q2 = w * (l3 + x * ex)
        q = q2 * lax.rsqrt(jnp.maximum(q2, 1e-36)) * rinv
        for c in range(3):
            hxyz[n, c] = q * s[c]
        hi = c3.astype(bf16)
        c3p[n, 0:128] = hi
        c3p[n, 128:256] = (c3 - hi.astype(f32)).astype(bf16)

    def beside(ns):
        return jnp.concatenate([c3p[n] for n in ns], axis=1) if len(ns) > 1 else c3p[ns[0]]

    def by_eight(x):
        return jnp.sum(x.reshape(4, 8, 128), axis=0)

    def dot_rows(h, m):
        return h[0] * m[0] + h[1] * m[1] + h[2] * m[2]

    def on_seconds(firsts):
        count = len(firsts[0][1])
        sums, parts = [None] * count, None
        for a, ns in firsts:
            part = jnp.dot(ms[a], beside(ns), preferred_element_type=f32)
            parts = part if parts is None else parts + part
        for a, ns in firsts:
            for g in range(4):
                rows = slice(32 * g, 32 * g + 32)
                m = [mi[a, rows, c * 128 : c * 128 + 128] for c in range(3)]
                for q in range(count):
                    h = [hxyz[ns[q], c, rows, :] for c in range(3)]
                    d = dot_rows(h, m)
                    add = [by_eight(h[c] * d) for c in range(3)]
                    sums[q] = add if sums[q] is None else [sums[q][c] + add[c] for c in range(3)]
        return [(sums[q], parts[:, q * 128 : q * 128 + 128]) for q in range(count)]

    def triple(tile):
        return [tile[4 + c : 5 + c] * 3.0 for c in range(3)]

    def on_firsts(firsts, tiles, rows_of_parts):
        mj = [triple(t) for t in tiles]
        for a, ns in firsts:
            g1[a] += lax.dot_general(
                rows_of_parts, beside(ns), (((1,), (1,)), ((), ())), preferred_element_type=f32)
        for a, ns in firsts:
            for g in range(4):
                rows = slice(32 * g, 32 * g + 32)
                sums = [f1[a, c, rows, :] for c in range(3)]
                for q, n in enumerate(ns):
                    h = [hxyz[n, c, rows, :] for c in range(3)]
                    d = dot_rows(h, mj[q])
                    sums = [sums[c] + h[c] * d for c in range(3)]
                for c in range(3):
                    f1[a, c, rows, :] = sums[c]

    def face_list(f):
        return [(face_first(f, p), [FACE + (f * 4 + p) * 4 + q for q in range(4)]) for p in range(4)]

    def edge_list(k):
        return [(edge_first(k, p), [EDGE + (k * 2 + p) * 2 + q for q in range(2)]) for p in range(2)]

    def corner_list(k):
        return [(corner_first(k), [CORNER + k])]

    kinds = ((0, 3, 4, 0, face_list, 1), (3, 9, 2, 12, edge_list, 6), (9, 13, 1, 24, corner_list, 4))

    def send_back(r, kind):
        low, high, count, start, entries, group = kinds[kind]

        def one(step, carry):
            for k in [step * group + u for u in range(group)]:
                fields = on_seconds(entries(k))
                for q in range(count):
                    back[r, start + k * count + q] = tile_field(*fields[q])
            return carry

        lax.fori_loop(0, (high - low) // group, one, 0)
        for m in range(low, high):
            fold_copy(r, m).start()

    def take_halo(r, kind):
        low, high, count, start, entries, group = kinds[kind]

        def one(step, carry):
            for k in [step * group + u for u in range(group)]:
                slots = [start + k * count + q for q in range(count)]
                parts = [mjp[s] for s in slots]
                wide = jnp.concatenate(parts, axis=1) if count > 1 else parts[0]
                on_firsts(entries(k), [halo[r, s] for s in slots], wide)
            return carry

        lax.fori_loop(0, (high - low) // group, one, 0)

    def own_tiles(r, seconds, firsts):
        def near(a):
            ns = [OWN + a * 4 + d for d in range(4)]
            bs = [lax.rem(a + d, 8) for d in range(4)]
            if seconds:
                two = jnp.dot(ms[a], beside(ns), preferred_element_type=f32)
            if firsts:
                mj = [triple(own[r, b]) for b in bs]
                wide = jnp.concatenate([ms[b, :, 0:128] for b in bs[1:]], axis=1)
                g1[a] = lax.dot_general(
                    wide, beside(ns[1:]), (((1,), (1,)), ((), ())), preferred_element_type=f32)
            sums = [[jnp.zeros((8, 128), f32)] * 3 for _ in range(4)]
            for g in range(4):
                rows = slice(32 * g, 32 * g + 32)
                m = [mi[a, rows, c * 128 : c * 128 + 128] for c in range(3)]
                first = None
                for d in range(4):
                    if d == 0 and not seconds:
                        continue
                    h = [hxyz[ns[d], c, rows, :] for c in range(3)]
                    if seconds:
                        t = dot_rows(h, m)
                        sums[d] = [sums[d][c] + by_eight(h[c] * t) for c in range(3)]
                    if firsts and d > 0:
                        t = dot_rows(h, mj[d])
                        add = [h[c] * t for c in range(3)]
                        first = add if first is None else [first[c] + add[c] for c in range(3)]
                if firsts:
                    for c in range(3):
                        f1[a, c, rows, :] = first[c]
            if seconds:
                vec[r, a] = tile_field(sums[0], two[:, 0:128])
                for d in range(1, 4):
                    for c in range(3):
                        f2own[bs[d], c] += sums[d][c]
                    g2own[bs[d]] += two[:, d * 128 : d * 128 + 128]

        def pair(k, carry):
            near(2 * k)
            near(2 * k + 1)
            return carry

        if seconds:
            f2own[...] = jnp.zeros_like(f2own)
            g2own[...] = jnp.zeros_like(g2own)
        lax.fori_loop(0, TILES // 2, pair, 0)
        for a in range(4):
            entry = [(a, [LAST + a])]
            if seconds:
                fields, parts = on_seconds(entry)[0]
                for c in range(3):
                    f2own[a + 4, c] += fields[c]
                g2own[a + 4] += parts
            if firsts:
                on_firsts(entry, [own[r, a + 4]], ms[a + 4, :, 0:128])

    def own_sums(r):
        total = jnp.zeros((8, 128), f32)
        for a in range(TILES):
            off = tile_field([f2own[a, c] for c in range(3)], g2own[a])
            total = total + own[r, a] * (vec[r, a] + 2.0 * off)
            vec[r, a] += off
        return total

    def wait_halo(r):
        for m in range(N_MSG):
            halo_copy(r, m).wait_recv()
        for slot in range(N_SLOTS):
            mjp[slot] = two_parts(halo[r, slot])

    def first_sums(r):
        for a in range(TILES):
            sums = [jnp.sum(jnp.transpose(f1[a, c]), axis=0, keepdims=True) for c in range(3)]
            parts = fold_parts(g1[a])
            vec[r, a] += put(*sums) - jnp.where(vec_rows, parts[:, :128] + parts[:, 128:], 0.0)

    def add_folded(r):
        for m in range(N_MSG):
            fold_copy(r, m).wait_recv()
        for slot in range(N_SLOTS):
            vec[r, SLOT_TILE[slot]] += fold[r, slot]

    def phase_copy(phase, k):
        return pltpu.make_async_remote_copy(
            src_ref=ar_send.at[phase], dst_ref=ar_recv.at[phase, k - 1],
            send_sem=as_sem.at[phase, k - 1], recv_sem=ar_sem.at[phase, k - 1],
            device_id=partner(phase, k), device_id_type=MESH)

    def start_phase(phase, total):
        ar_send[phase] = total
        for k in range(1, 8):
            phase_copy(phase, k).start()

    def end_phase(phase):
        total = ar_send[phase]
        for k in range(1, 8):
            phase_copy(phase, k).wait_recv()
            total = total + ar_recv[phase, k - 1]
        return total

    def rows_dot(left, right):
        total = left[0] * right[0]
        for a in range(1, TILES):
            total = total + left[a] * right[a]
        return total

    columns(0)

    def own_near(a, carry):
        for d in range(4):
            coefficients(OWN + a * 4 + d, a, own[0, lax.rem(a + d, 8)], True)
        return carry

    lax.fori_loop(0, 8, own_near, 0)
    for a in range(4):
        coefficients(LAST + a, a, own[0, a + 4], True)
    wait_halo(0)
    for e, start, count in MESSAGES:
        shift = jnp.where(row == 0, e[0] * BOX_EDGE, 0.0) + jnp.where(
            row == 1, e[1] * BOX_EDGE, 0.0) + jnp.where(row == 2, e[2] * BOX_EDGE, 0.0)
        for slot in range(start, start + count):
            xj[slot] = halo[0, slot] + shift

    def face_one(n, carry):
        f = n // 4
        for q in range(4):
            coefficients(FACE + n * 4 + q, face_first(f, n % 4), xj[f * 4 + q], False)
        return carry

    def edge_one(k, carry):
        for p in range(2):
            for q in range(2):
                coefficients(EDGE + k * 4 + p * 2 + q, edge_first(k, p), xj[12 + k * 2 + q], False)
        return carry

    for k in range(4):
        coefficients(CORNER + k, corner_first(k), xj[24 + k], False)
    send_back(0, 2)
    lax.fori_loop(0, 6, edge_one, 0)
    send_back(0, 1)
    lax.fori_loop(0, 12, face_one, 0)
    send_back(0, 0)
    own_tiles(0, True, True)
    own_sums(0)
    for kind in range(3):
        take_halo(0, kind)
    first_sums(0)
    add_folded(0)

    for r in (1, 2):
        for a in range(TILES):
            own[r, a] = polar8[a] * vec[r - 1, a]
        send_halo(r)
        columns(r)
        for kind in (2, 1, 0):
            send_back(r, kind)
        own_tiles(r, True, r == 1)
        g12 = own_sums(r)
        wait_halo(r)
        if r == 2:
            for slot in range(N_SLOTS):
                g12 = g12 + 2.0 * (halo[2, slot] * back[2, slot])
            parts = [
                rows_dot(vec[0], own[1]), rows_dot(vec[1], own[1]), rows_dot(vec[1], own[2]), g12]
            parts = [jnp.sum(jnp.sum(g, axis=0, keepdims=True), axis=1, keepdims=True) for g in parts]
            lane = lax.broadcasted_iota(jnp.int32, (1, 128), 1)
            start_phase(0, jnp.where(lane == 0, parts[0], jnp.where(
                lane == 1, parts[1], jnp.where(lane == 2, parts[2], parts[3]))))
            own_tiles(2, False, True)
        take_halo(r, 0)
        if r == 2:
            start_phase(1, end_phase(0))
        take_halo(r, 1)
        take_halo(r, 2)
        first_sums(r)
        if r == 2:
            start_phase(2, end_phase(1))
        add_folded(r)

    sums = end_phase(2)
    s00, s01, s11, s12 = (sums[:, i : i + 1] for i in range(4))
    alpha = s00 / (s00 - s01)
    keep = 1.0 - alpha
    rho = keep * keep * s00 + 2.0 * keep * alpha * s01 + alpha * alpha * s11
    a0 = keep + rho / s00
    a1 = alpha
    denom = (a0 * a0 * s00 + 2.0 * a0 * a1 * s01 + a1 * a1 * s11) - (
        a0 * a0 * s01 + 2.0 * a0 * a1 * s11 + a1 * a1 * s12)
    step = rho / denom
    d0 = 1.0 / SCALE
    d1, d2 = (alpha + step * a0) * d0, step * a1 * d0
    r0, r1, r2 = keep - step * a0, alpha - step * a1 + step * a0, step * a1
    for a in range(TILES):
        dip = d0 * own[0, a] + d1 * own[1, a] + d2 * own[2, a]
        res = r0 * vec[0, a] + r1 * vec[1, a] + r2 * vec[2, a]
        for c in range(3):
            out[0, 8 * c + a : 8 * c + a + 1] = dip[4 + c : 5 + c]
            out[1, 8 * c + a : 8 * c + a + 1] = res[4 + c : 5 + c]

    for r in range(3):
        for m in range(N_MSG):
            halo_copy(r, m).wait_send()
            fold_copy(r, m).wait_send()
    for phase in range(3):
        for k in range(1, 8):
            phase_copy(phase, k).wait_send()


def solution(mesh):
    sizes = tuple(mesh.shape[a] for a in AXES)
    f32, bf16 = jnp.float32, jnp.bfloat16

    def shards(positions, polar, field, groups, pair_tiles):
        vmem = pl.BlockSpec(memory_space=pltpu.VMEM)
        anywhere = pl.BlockSpec(memory_space=pl.ANY)
        dma = pltpu.SemaphoreType.DMA
        atoms = positions.shape[-1]
        rows = atoms // TILE
        scratch = [
            pltpu.VMEM((3 * rows, TILE), f32),
            pltpu.VMEM((rows, TILE), f32),
            pltpu.VMEM((3 * rows, TILE), f32),
            pltpu.VMEM((rows, TILE), jnp.int32),
            pltpu.VMEM((3, 1, pair_tiles.shape[-1]), jnp.int32),
            pltpu.VMEM((ENTRIES, 128), jnp.int32),
            pltpu.VMEM((ENTRIES, 3, 128, 128), f32),
            pltpu.VMEM((ENTRIES, 256, 128), bf16),
            pltpu.VMEM((8, 128, 640), f32),
            pltpu.VMEM((8, 128, 384), f32),
            pltpu.VMEM((8, 16, 256), bf16),
            pltpu.VMEM((N_SLOTS, 16, 128), bf16),
            pltpu.VMEM((8, 3, 128, 128), f32),
            pltpu.VMEM((8, 16, 256), f32),
            pltpu.VMEM((8, 3, 8, 128), f32),
            pltpu.VMEM((8, 16, 128), f32),
            pltpu.VMEM((ENTRIES, 128), f32),
            pltpu.VMEM((N_SLOTS, 8, 128), f32),
            pltpu.VMEM((3, 8, 8, 128), f32),
            pltpu.VMEM((3, 8, 8, 128), f32),
            pltpu.VMEM((8, 8, 128), f32),
            pltpu.VMEM((3, N_SLOTS, 8, 128), f32),
            pltpu.VMEM((3, N_SLOTS, 8, 128), f32),
            pltpu.VMEM((3, N_SLOTS, 8, 128), f32),
            pltpu.VMEM((3, N_SLOTS, 8, 128), f32),
            pltpu.VMEM((3, 1, 128), f32),
            pltpu.VMEM((3, 7, 1, 128), f32),
            dma((6,)),
            dma((3, N_MSG)), dma((3, N_MSG)), dma((3, N_MSG)), dma((3, N_MSG)),
            dma((3, 7)), dma((3, 7)),
        ]
        out = pl.pallas_call(
            functools.partial(kernel, sizes),
            out_shape=jax.ShapeDtypeStruct((2, 3 * rows, TILE), f32),
            in_specs=[anywhere] * 6,
            out_specs=vmem,
            scratch_shapes=scratch,
            compiler_params=pltpu.CompilerParams(
                collective_id=0, has_side_effects=True, vmem_limit_bytes=64 * 1024 * 1024),
            name="dipole_cg",
        )(positions.reshape(3 * rows, TILE), polar.reshape(rows, TILE), field.reshape(3 * rows, TILE),
          groups.reshape(rows, TILE), pair_tiles.reshape(3, 1, -1), jnp.asarray(KEYS))
        return out[0].reshape(1, 1, 1, 3, atoms), out[1].reshape(1, 1, 1, 3, atoms)

    placed = (
        P(*AXES, None, None), P(*AXES, None), P(*AXES, None, None), P(*AXES, None), P(*AXES, None, None))
    return jax.shard_map(
        shards, mesh=mesh, in_specs=placed, out_specs=(placed[0], placed[0]), check_vma=False)
```

```python
import functools

import jax
import jax.numpy as jnp
import numpy as np
from jax import lax
from jax.experimental import pallas as pl
from jax.experimental.pallas import tpu as pltpu
from jax.sharding import PartitionSpec as P

TILE = 128
TILES = 8
AXES = ("gx", "gy", "gz")
BOX_EDGE = 21.7
THOLE_A = 0.39
FAR = 1000.0
SCALE = 3.0 / 16.0
C10 = np.float32(10.0 / 3.0)
C8 = np.float32(5.0) - (C10 - np.float32(1.0))
MESH = pl.DeviceIdType.MESH
SHELL = [
    (0, 0, 0), (0, 0, 1), (0, 1, -1), (0, 1, 0), (0, 1, 1), (1, -1, -1), (1, -1, 0),
    (1, -1, 1), (1, 0, -1), (1, 0, 0), (1, 0, 1), (1, 1, -1), (1, 1, 0), (1, 1, 1),
]
N_SLOTS = 28
FACE, EDGE, CORNER, OWN, LAST = 0, 48, 72, 76, 108
ENTRIES = 112


def face_first(f, p):
    s = 1 + f + f * (f - 1) // 2
    return p // s * (2 * s) + s + p % s


def edge_first(k, p):
    g, sg = k // 2, k % 2
    free = 4 - 2 * g + g * (g - 1) // 2
    return free * p + 4 - 2 * ((2 - g) // 2) + (1 + g // 2) * sg


def corner_first(k):
    return 4 + k


def tables():
    messages, slot_tile, keys = [], [], []
    for f in range(3):
        s = 1 << f
        e = [0, 0, 0]
        e[2 - f] = 1
        messages.append((tuple(e), len(slot_tile), 4))
        slot_tile += [q // s * 2 * s + q % s for q in range(4)]
    for k in range(6):
        g, sg = k // 2, k % 2
        e = [[0, 1, 2 * sg - 1], [1, 0, 2 * sg - 1], [1, 2 * sg - 1, 0]][g]
        free, low = (4, 2, 1)[g], (1, 1, 2)[g]
        messages.append((tuple(e), len(slot_tile), 2))
        slot_tile += [free * q + low * (1 - sg) for q in range(2)]
    for k in range(4):
        sy, sz = k // 2, k % 2
        messages.append(((1, 2 * sy - 1, 2 * sz - 1), len(slot_tile), 1))
        slot_tile += [2 * (1 - sy) + 1 - sz]
    for m, (e, start, count) in enumerate(messages):
        for p in range(count):
            if m < 3:
                a = face_first(m, p)
            elif m < 9:
                a = edge_first(m - 3, p)
            else:
                a = corner_first(m - 9)
            keys += [(a, SHELL.index(e), slot_tile[start + q]) for q in range(count)]
    for a in range(8):
        for d in range(4):
            b = (a + d) % 8
            keys.append((min(a, b), 0, max(a, b)))
    keys += [(a, 0, a + 4) for a in range(4)]
    assert len(set(keys)) == ENTRIES
    key = np.array([a * 128 + c * 8 + b for a, c, b in keys], np.int32)
    return messages, slot_tile, np.ascontiguousarray(np.broadcast_to(key[:, None], (ENTRIES, 128)))


MESSAGES, SLOT_TILE, KEYS = tables()
N_MSG = len(MESSAGES)


def halves(tile):
    hi = tile.astype(jnp.bfloat16).astype(jnp.float32)
    return hi, (tile - hi)


def two_parts(tile):
    hi, rest = halves(tile)
    return jnp.concatenate([hi, rest], axis=0).astype(jnp.bfloat16)


def fold_parts(parts):
    return parts[0:8] + parts[8:16]


def kernel(sizes, pos_in, pol_in, fld_in, grp_in, prs_in, keys_in, out,
           pos, pol, fld, grp, prs, keys, hxyz, c3p, xi, mi, ms, mjp, f1, g1, f2own, g2own, flag, xj,
           own, vec, polar8, send, halo, back, fold, ar_send, ar_recv,
           in_sem, hs_sem, hr_sem, fs_sem, fr_sem, as_sem, ar_sem):
    f32, bf16 = jnp.float32, jnp.bfloat16
    me = tuple(lax.axis_index(a) for a in AXES)
    gx, gy, gz = me

    def at(e):
        return tuple(lax.rem(m + d + n, n) for m, d, n in zip(me, e, sizes))

    core, zed = lax.rem(gy, 2), gy // 2

    def partner(phase, k):
        if phase == 0:
            j = lax.rem(core * 4 + gz + k, 8)
            return (gx, gy - core + j // 4, lax.rem(j, 4))
        if phase == 1:
            return (lax.rem(gx + k, 8), gy, gz)
        return (gx, lax.rem(zed + k, 8) * 2 + core, gz)

    arguments = (pos_in, pol_in, fld_in, grp_in, prs_in, keys_in)
    taken = [
        pltpu.make_async_copy(src, dst, in_sem.at[i])
        for i, (src, dst) in enumerate(zip(arguments, (pos, pol, fld, grp, prs, keys)))]
    for copy in taken:
        copy.start()

    barrier = pltpu.get_barrier_semaphore()
    signals = 0
    for e, _, _ in MESSAGES:
        for sign in (1, -1):
            pl.semaphore_signal(barrier, inc=1, device_id=at(tuple(sign * d for d in e)), device_id_type=MESH)
            signals += 1
    for phase in range(3):
        for k in range(1, 8):
            pl.semaphore_signal(barrier, inc=1, device_id=partner(phase, k), device_id_type=MESH)
            signals += 1

    row = lax.broadcasted_iota(jnp.int32, (8, 128), 0)
    vec_rows = jnp.logical_and(row >= 4, row < 7)

    def put(x, y, z):
        return jnp.where(row == 4, x, jnp.where(row == 5, y, jnp.where(row == 6, z, 0.0)))

    def tile_field(sums, parts):
        rows = [jnp.sum(f, axis=0, keepdims=True) for f in sums]
        return put(*rows) - jnp.where(vec_rows, fold_parts(parts), 0.0)

    for copy in taken:
        copy.wait()

    for a in range(TILES):
        p = pol[a : a + 1]
        polar8[a] = jnp.broadcast_to(p * SCALE, (8, 128))
        own[0, a] = jnp.concatenate(
            [pos[8 * c + a : 8 * c + a + 1] for c in range(3)] + [lax.rsqrt(p)]
            + [p * SCALE * fld[8 * c + a : 8 * c + a + 1] for c in range(3)]
            + [grp[a : a + 1].astype(f32)], axis=0)

    def halo_copy(r, m):
        e, start, count = MESSAGES[m]
        return pltpu.make_async_remote_copy(
            src_ref=send.at[r, pl.ds(start, count)], dst_ref=halo.at[r, pl.ds(start, count)],
            send_sem=hs_sem.at[r, m], recv_sem=hr_sem.at[r, m],
            device_id=at(tuple(-d for d in e)), device_id_type=MESH)

    def fold_copy(r, m):
        e, start, count = MESSAGES[m]
        return pltpu.make_async_remote_copy(
            src_ref=back.at[r, pl.ds(start, count)], dst_ref=fold.at[r, pl.ds(start, count)],
            send_sem=fs_sem.at[r, m], recv_sem=fr_sem.at[r, m],
            device_id=at(e), device_id_type=MESH)

    def send_halo(r):
        for slot in range(N_SLOTS):
            send[r, slot] = own[r, SLOT_TILE[slot]]
        if r == 0:
            pl.semaphore_wait(barrier, signals)
        for m in reversed(range(N_MSG)):
            halo_copy(r, m).start()

    send_halo(0)

    key_row = prs[0] * 128 + prs[1] * 8 + prs[2]
    hit = jnp.where(keys[:, : key_row.shape[1]] == key_row, 0.0, FAR)
    flag[...] = jnp.broadcast_to(jnp.min(hit, axis=1, keepdims=True), (ENTRIES, 128))

    def columns(r):
        cols = jnp.transpose(own[r].reshape(64, 128))
        for a in range(TILES):
            def wide(k, scale):
                return jnp.broadcast_to(cols[:, a * 8 + k : a * 8 + k + 1] * scale, (128, 128))

            for c in range(3):
                mi[a, :, c * 128 : c * 128 + 128] = wide(4 + c, 3.0)
            if r == 0:
                for c in range(3):
                    xi[a, :, c * 128 : c * 128 + 128] = wide(c, 1.0)
                xi[a, :, 384:512] = wide(3, -THOLE_A)
                xi[a, :, 512:640] = wide(7, 1.0)
            parts = two_parts(own[r, a])
            ms[a] = jnp.concatenate([parts, parts], axis=1)

    def coefficients(n, a, tile, grouped):
        shift = flag[pl.ds(n, 1), :]
        xs = [tile[c : c + 1] for c in range(4)]
        xs[0] = xs[0] + shift
        group = tile[7:8]
        s = [xs[c] - xi[a, :, c * 128 : c * 128 + 128] for c in range(3)]
        r2 = s[0] * s[0] + s[1] * s[1] + s[2] * s[2]
        if grouped:
            r2 = jnp.where(xi[a, :, 512:640] == group, FAR * FAR, r2)
        rinv = lax.rsqrt(r2)
        r = r2 * rinv
        x = r2 * r * (xi[a, :, 384:512] * xs[3])
        ex = jnp.exp(x)
        l3 = 1.0 - ex
        v = jnp.clip(r - 8.0, -1.0, 1.0)
        v2 = v * v
        cut = jnp.maximum(C8 - v * ((v2 - C10) * v2 + 5.0), 0.0)
        w = cut * (rinv * rinv * rinv)
        c3 = w * l3
        q2 = w * (l3 + x * ex)
        q = q2 * lax.rsqrt(jnp.maximum(q2, 1e-36)) * rinv
        for c in range(3):
            hxyz[n, c] = q * s[c]
        hi = c3.astype(bf16)
        c3p[n, 0:128] = hi
        c3p[n, 128:256] = (c3 - hi.astype(f32)).astype(bf16)

    def beside(ns):
        return jnp.concatenate([c3p[n] for n in ns], axis=1) if len(ns) > 1 else c3p[ns[0]]

    def by_eight(x):
        return jnp.sum(x.reshape(4, 8, 128), axis=0)

    def dot_rows(h, m):
        return h[0] * m[0] + h[1] * m[1] + h[2] * m[2]

    def on_seconds(firsts):
        count = len(firsts[0][1])
        sums, parts = [None] * count, None
        for a, ns in firsts:
            part = jnp.dot(ms[a], beside(ns), preferred_element_type=f32)
            parts = part if parts is None else parts + part
        for a, ns in firsts:
            for g in range(4):
                rows = slice(32 * g, 32 * g + 32)
                m = [mi[a, rows, c * 128 : c * 128 + 128] for c in range(3)]
                for q in range(count):
                    h = [hxyz[ns[q], c, rows, :] for c in range(3)]
                    d = dot_rows(h, m)
                    add = [by_eight(h[c] * d) for c in range(3)]
                    sums[q] = add if sums[q] is None else [sums[q][c] + add[c] for c in range(3)]
        return [(sums[q], parts[:, q * 128 : q * 128 + 128]) for q in range(count)]

    def triple(tile):
        return [tile[4 + c : 5 + c] * 3.0 for c in range(3)]

    def on_firsts(firsts, tiles, rows_of_parts):
        mj = [triple(t) for t in tiles]
        for a, ns in firsts:
            g1[a] += lax.dot_general(
                rows_of_parts, beside(ns), (((1,), (1,)), ((), ())), preferred_element_type=f32)
        for a, ns in firsts:
            for g in range(4):
                rows = slice(32 * g, 32 * g + 32)
                sums = [f1[a, c, rows, :] for c in range(3)]
                for q, n in enumerate(ns):
                    h = [hxyz[n, c, rows, :] for c in range(3)]
                    d = dot_rows(h, mj[q])
                    sums = [sums[c] + h[c] * d for c in range(3)]
                for c in range(3):
                    f1[a, c, rows, :] = sums[c]

    def face_list(f):
        return [(face_first(f, p), [FACE + (f * 4 + p) * 4 + q for q in range(4)]) for p in range(4)]

    def edge_list(k):
        return [(edge_first(k, p), [EDGE + (k * 2 + p) * 2 + q for q in range(2)]) for p in range(2)]

    def corner_list(k):
        return [(corner_first(k), [CORNER + k])]

    kinds = ((0, 3, 4, 0, face_list, 1), (3, 9, 2, 12, edge_list, 6), (9, 13, 1, 24, corner_list, 4))

    def send_back(r, kind):
        low, high, count, start, entries, group = kinds[kind]

        def one(step, carry):
            for k in [step * group + u for u in range(group)]:
                fields = on_seconds(entries(k))
                for q in range(count):
                    back[r, start + k * count + q] = tile_field(*fields[q])
            return carry

        lax.fori_loop(0, (high - low) // group, one, 0)
        for m in range(low, high):
            fold_copy(r, m).start()

    def take_halo(r, kind):
        low, high, count, start, entries, group = kinds[kind]

        def one(step, carry):
            for k in [step * group + u for u in range(group)]:
                slots = [start + k * count + q for q in range(count)]
                parts = [mjp[s] for s in slots]
                wide = jnp.concatenate(parts, axis=1) if count > 1 else parts[0]
                on_firsts(entries(k), [halo[r, s] for s in slots], wide)
            return carry

        lax.fori_loop(0, (high - low) // group, one, 0)

    def own_tiles(r, seconds, firsts):
        def near(a):
            ns = [OWN + a * 4 + d for d in range(4)]
            bs = [lax.rem(a + d, 8) for d in range(4)]
            if seconds:
                two = jnp.dot(ms[a], beside(ns), preferred_element_type=f32)
            if firsts:
                mj = [triple(own[r, b]) for b in bs]
                wide = jnp.concatenate([ms[b, :, 0:128] for b in bs[1:]], axis=1)
                g1[a] = lax.dot_general(
                    wide, beside(ns[1:]), (((1,), (1,)), ((), ())), preferred_element_type=f32)
            sums = [[jnp.zeros((8, 128), f32)] * 3 for _ in range(4)]
            for g in range(4):
                rows = slice(32 * g, 32 * g + 32)
                m = [mi[a, rows, c * 128 : c * 128 + 128] for c in range(3)]
                first = None
                for d in range(4):
                    if d == 0 and not seconds:
                        continue
                    h = [hxyz[ns[d], c, rows, :] for c in range(3)]
                    if seconds:
                        t = dot_rows(h, m)
                        sums[d] = [sums[d][c] + by_eight(h[c] * t) for c in range(3)]
                    if firsts and d > 0:
                        t = dot_rows(h, mj[d])
                        add = [h[c] * t for c in range(3)]
                        first = add if first is None else [first[c] + add[c] for c in range(3)]
                if firsts:
                    for c in range(3):
                        f1[a, c, rows, :] = first[c]
            if seconds:
                vec[r, a] = tile_field(sums[0], two[:, 0:128])
                for d in range(1, 4):
                    for c in range(3):
                        f2own[bs[d], c] += sums[d][c]
                    g2own[bs[d]] += two[:, d * 128 : d * 128 + 128]

        def pair(k, carry):
            near(2 * k)
            near(2 * k + 1)
            return carry

        if seconds:
            f2own[...] = jnp.zeros_like(f2own)
            g2own[...] = jnp.zeros_like(g2own)
        lax.fori_loop(0, TILES // 2, pair, 0)
        for a in range(4):
            entry = [(a, [LAST + a])]
            if seconds:
                fields, parts = on_seconds(entry)[0]
                for c in range(3):
                    f2own[a + 4, c] += fields[c]
                g2own[a + 4] += parts
            if firsts:
                on_firsts(entry, [own[r, a + 4]], ms[a + 4, :, 0:128])

    def own_sums(r):
        total = jnp.zeros((8, 128), f32)
        for a in range(TILES):
            off = tile_field([f2own[a, c] for c in range(3)], g2own[a])
            total = total + own[r, a] * (vec[r, a] + 2.0 * off)
            vec[r, a] += off
        return total

    def wait_halo(r):
        for m in range(N_MSG):
            halo_copy(r, m).wait_recv()
        for slot in range(N_SLOTS):
            mjp[slot] = two_parts(halo[r, slot])

    def first_sums(r):
        for a in range(TILES):
            sums = [jnp.sum(jnp.transpose(f1[a, c]), axis=0, keepdims=True) for c in range(3)]
            parts = fold_parts(g1[a])
            vec[r, a] += put(*sums) - jnp.where(vec_rows, parts[:, :128] + parts[:, 128:], 0.0)

    def add_folded(r):
        for m in range(N_MSG):
            fold_copy(r, m).wait_recv()
        for slot in range(N_SLOTS):
            vec[r, SLOT_TILE[slot]] += fold[r, slot]

    def phase_copy(phase, k):
        return pltpu.make_async_remote_copy(
            src_ref=ar_send.at[phase], dst_ref=ar_recv.at[phase, k - 1],
            send_sem=as_sem.at[phase, k - 1], recv_sem=ar_sem.at[phase, k - 1],
            device_id=partner(phase, k), device_id_type=MESH)

    def start_phase(phase, total):
        ar_send[phase] = total
        for k in (4, 3, 5, 2, 6, 1, 7):
            phase_copy(phase, k).start()

    def end_phase(phase):
        total = ar_send[phase]
        for k in range(1, 8):
            phase_copy(phase, k).wait_recv()
            total = total + ar_recv[phase, k - 1]
        return total

    def rows_dot(left, right):
        total = left[0] * right[0]
        for a in range(1, TILES):
            total = total + left[a] * right[a]
        return total

    columns(0)

    def own_near(a, carry):
        for d in range(4):
            coefficients(OWN + a * 4 + d, a, own[0, lax.rem(a + d, 8)], True)
        return carry

    lax.fori_loop(0, 8, own_near, 0)
    for a in range(4):
        coefficients(LAST + a, a, own[0, a + 4], True)
    wait_halo(0)
    for e, start, count in MESSAGES:
        shift = jnp.where(row == 0, e[0] * BOX_EDGE, 0.0) + jnp.where(
            row == 1, e[1] * BOX_EDGE, 0.0) + jnp.where(row == 2, e[2] * BOX_EDGE, 0.0)
        for slot in range(start, start + count):
            xj[slot] = halo[0, slot] + shift

    def face_one(n, carry):
        f = n // 4
        for q in range(4):
            coefficients(FACE + n * 4 + q, face_first(f, n % 4), xj[f * 4 + q], False)
        return carry

    def edge_one(k, carry):
        for p in range(2):
            for q in range(2):
                coefficients(EDGE + k * 4 + p * 2 + q, edge_first(k, p), xj[12 + k * 2 + q], False)
        return carry

    for k in range(4):
        coefficients(CORNER + k, corner_first(k), xj[24 + k], False)
    send_back(0, 2)
    lax.fori_loop(0, 6, edge_one, 0)
    send_back(0, 1)
    lax.fori_loop(0, 12, face_one, 0)
    send_back(0, 0)
    own_tiles(0, True, True)
    own_sums(0)
    for kind in range(3):
        take_halo(0, kind)
    first_sums(0)
    add_folded(0)

    for r in (1, 2):
        for a in range(TILES):
            own[r, a] = polar8[a] * vec[r - 1, a]
        send_halo(r)
        columns(r)
        for kind in (2, 1, 0):
            send_back(r, kind)
        own_tiles(r, True, r == 1)
        g12 = own_sums(r)
        wait_halo(r)
        if r == 2:
            for slot in range(N_SLOTS):
                g12 = g12 + 2.0 * (halo[2, slot] * back[2, slot])
            parts = [
                rows_dot(vec[0], own[1]), rows_dot(vec[1], own[1]), rows_dot(vec[1], own[2]), g12]
            parts = [jnp.sum(jnp.sum(g, axis=0, keepdims=True), axis=1, keepdims=True) for g in parts]
            lane = lax.broadcasted_iota(jnp.int32, (1, 128), 1)
            start_phase(0, jnp.where(lane == 0, parts[0], jnp.where(
                lane == 1, parts[1], jnp.where(lane == 2, parts[2], parts[3]))))
            own_tiles(2, False, True)
        take_halo(r, 1)
        take_halo(r, 2)
        if r == 2:
            start_phase(1, end_phase(0))
        take_halo(r, 0)
        first_sums(r)
        if r == 2:
            start_phase(2, end_phase(1))
        add_folded(r)

    sums = end_phase(2)
    s00, s01, s11, s12 = (sums[:, i : i + 1] for i in range(4))
    alpha = s00 / (s00 - s01)
    keep = 1.0 - alpha
    rho = keep * keep * s00 + 2.0 * keep * alpha * s01 + alpha * alpha * s11
    a0 = keep + rho / s00
    a1 = alpha
    denom = (a0 * a0 * s00 + 2.0 * a0 * a1 * s01 + a1 * a1 * s11) - (
        a0 * a0 * s01 + 2.0 * a0 * a1 * s11 + a1 * a1 * s12)
    step = rho / denom
    d0 = 1.0 / SCALE
    d1, d2 = (alpha + step * a0) * d0, step * a1 * d0
    r0, r1, r2 = keep - step * a0, alpha - step * a1 + step * a0, step * a1
    for a in range(TILES):
        dip = d0 * own[0, a] + d1 * own[1, a] + d2 * own[2, a]
        res = r0 * vec[0, a] + r1 * vec[1, a] + r2 * vec[2, a]
        for c in range(3):
            out[0, 8 * c + a : 8 * c + a + 1] = dip[4 + c : 5 + c]
            out[1, 8 * c + a : 8 * c + a + 1] = res[4 + c : 5 + c]

    for r in range(3):
        for m in range(N_MSG):
            halo_copy(r, m).wait_send()
            fold_copy(r, m).wait_send()
    for phase in range(3):
        for k in range(1, 8):
            phase_copy(phase, k).wait_send()


def solution(mesh):
    sizes = tuple(mesh.shape[a] for a in AXES)
    f32, bf16 = jnp.float32, jnp.bfloat16

    def shards(positions, polar, field, groups, pair_tiles):
        vmem = pl.BlockSpec(memory_space=pltpu.VMEM)
        anywhere = pl.BlockSpec(memory_space=pl.ANY)
        dma = pltpu.SemaphoreType.DMA
        atoms = positions.shape[-1]
        rows = atoms // TILE
        scratch = [
            pltpu.VMEM((3 * rows, TILE), f32),
            pltpu.VMEM((rows, TILE), f32),
            pltpu.VMEM((3 * rows, TILE), f32),
            pltpu.VMEM((rows, TILE), jnp.int32),
            pltpu.VMEM((3, 1, pair_tiles.shape[-1]), jnp.int32),
            pltpu.VMEM((ENTRIES, 128), jnp.int32),
            pltpu.VMEM((ENTRIES, 3, 128, 128), f32),
            pltpu.VMEM((ENTRIES, 256, 128), bf16),
            pltpu.VMEM((8, 128, 640), f32),
            pltpu.VMEM((8, 128, 384), f32),
            pltpu.VMEM((8, 16, 256), bf16),
            pltpu.VMEM((N_SLOTS, 16, 128), bf16),
            pltpu.VMEM((8, 3, 128, 128), f32),
            pltpu.VMEM((8, 16, 256), f32),
            pltpu.VMEM((8, 3, 8, 128), f32),
            pltpu.VMEM((8, 16, 128), f32),
            pltpu.VMEM((ENTRIES, 128), f32),
            pltpu.VMEM((N_SLOTS, 8, 128), f32),
            pltpu.VMEM((3, 8, 8, 128), f32),
            pltpu.VMEM((3, 8, 8, 128), f32),
            pltpu.VMEM((8, 8, 128), f32),
            pltpu.VMEM((3, N_SLOTS, 8, 128), f32),
            pltpu.VMEM((3, N_SLOTS, 8, 128), f32),
            pltpu.VMEM((3, N_SLOTS, 8, 128), f32),
            pltpu.VMEM((3, N_SLOTS, 8, 128), f32),
            pltpu.VMEM((3, 1, 128), f32),
            pltpu.VMEM((3, 7, 1, 128), f32),
            dma((6,)),
            dma((3, N_MSG)), dma((3, N_MSG)), dma((3, N_MSG)), dma((3, N_MSG)),
            dma((3, 7)), dma((3, 7)),
        ]
        out = pl.pallas_call(
            functools.partial(kernel, sizes),
            out_shape=jax.ShapeDtypeStruct((2, 3 * rows, TILE), f32),
            in_specs=[anywhere] * 6,
            out_specs=vmem,
            scratch_shapes=scratch,
            compiler_params=pltpu.CompilerParams(
                collective_id=0, has_side_effects=True, vmem_limit_bytes=64 * 1024 * 1024),
            name="dipole_cg",
        )(positions.reshape(3 * rows, TILE), polar.reshape(rows, TILE), field.reshape(3 * rows, TILE),
          groups.reshape(rows, TILE), pair_tiles.reshape(3, 1, -1), jnp.asarray(KEYS))
        return out[0].reshape(1, 1, 1, 3, atoms), out[1].reshape(1, 1, 1, 3, atoms)

    placed = (
        P(*AXES, None, None), P(*AXES, None), P(*AXES, None, None), P(*AXES, None), P(*AXES, None, None))
    return jax.shard_map(
        shards, mesh=mesh, in_specs=placed, out_specs=(placed[0], placed[0]), check_vma=False)
```
